32 devices in a mesh: ctx: 8 (over z, core), vocab: 4 (over y, x).
Axes of the slice: x: 2, y: 2, z: 4, core: 2. Of those that a mesh axis runs over, the one named last changes fastest.
Arguments:
- hidden_in: bfloat16 [1024, 4096], P('ctx'), may hold values from -128 to 128
- attn_gain: float32 [4096], replicated, may hold values from 0.1 to 1.9
- w_query: bfloat16 [4096, 4096], P(None, 'vocab'), may hold values from -2 to 2
- w_key: bfloat16 [4096, 1024], P(None, 'vocab'), may hold values from -2 to 2
- w_value: bfloat16 [4096, 1024], P(None, 'vocab'), may hold values from -0.09375 to 0.09375
- w_out: bfloat16 [4096, 4096], P('vocab'), may hold values from -0.5 to 0.5
- final_gain: float32 [4096], replicated, may hold values from 0.5 to 1.5
- teacher_head: bfloat16 [65536, 4096], P(('vocab', 'ctx')), may hold values from -18 to 18
- draft_rows: bfloat16 [1024, 2048], P('ctx'), may hold values from -1.5 to 1.5
- draft_head: bfloat16 [65536, 2048], P(('vocab', 'ctx')), may hold values from -64 to 64
- target_ids: int32 [1024], replicated, may hold values from 0 to 65535
- rollout_lengths: int32 [4], replicated, may hold values from 1 to 512, 1024 in all
- stretch_order: int32 [16], replicated, may hold values from 0 to 15, as said below
Outputs:
- draft_grad: float32 [1024, 2048], P('ctx', 'vocab')
The draws below stay inside these ranges and needn't reach their ends.
Inputs may be any that keep to these rules, and one draw needn't show every extreme that they name: `rollout_lengths`: the lengths add up to 1024. `stretch_order`: each block number appears once; entries 2c and 2c + 1 add up to 15.
All inputs are finite; a program needn't handle non-finite values.
Results may differ from the reference program's by a relative error of at most 0.0045.
Values may be sent and summed in bfloat16 or wider, within the bound.
A program may use at most 128 MiB of HBM per device.

```python
import math
import jax
import jax.numpy as jnp
import numpy as np
from jax import lax

D = 4096
HEADS = 32
KV_HEADS = 8
HEAD_DIM = 128
DD = 2048
VOCAB = 65536
ROLLOUTS = 4
TOK_DEV = 128
TOKENS = 1024
STRETCHES = 16
N_CTX = 8


def draw_hidden_in(key, part):
    column_scale = 1.0 + 2.0 * jnp.arange(D, dtype=jnp.float32) / (D - 1)
    values = jnp.clip(jax.random.normal(jax.random.fold_in(key, 4), (TOKENS, D), jnp.float32), -6.0, 6.0) * column_scale[None, :]
    return values.astype(jnp.bfloat16)


def draw_w_query(key, part):
    values = jnp.clip(jax.random.normal(jax.random.fold_in(key, 5), (D, HEADS * HEAD_DIM), jnp.float32), -6.0, 6.0) / math.sqrt(D)
    return jnp.clip(values, -2.0, 2.0).astype(jnp.bfloat16)


def draw_w_key(key, part):
    values = jnp.clip(jax.random.normal(jax.random.fold_in(key, 6), (D, KV_HEADS * HEAD_DIM), jnp.float32), -6.0, 6.0) / math.sqrt(D)
    return jnp.clip(values, -2.0, 2.0).astype(jnp.bfloat16)


def boosted_rows(key, rows, width, spread, limit):
    values = jnp.clip(jax.random.normal(jax.random.fold_in(key, 7), (rows, width), jnp.float32), -6.0, 6.0) * spread
    return jnp.clip(values, -limit, limit).astype(jnp.bfloat16)


def draw_teacher_head(key, part):
    return boosted_rows(key, VOCAB, D, 3.0 / math.sqrt(D), 18.0)


def draw_draft_head(key, part):
    return boosted_rows(jax.random.fold_in(key, 13), VOCAB, DD, 12.0 / math.sqrt(DD), 64.0)


def draw_stretch_order(key, part):
    pair_count = STRETCHES // 2
    order = jax.random.permutation(jax.random.fold_in(key, 11), pair_count).astype(jnp.int32)
    flips = jax.random.randint(jax.random.fold_in(key, 12), (pair_count,), 0, 2)
    leading = jnp.where(flips == 1, STRETCHES - 1 - order, order)
    trailing = STRETCHES - 1 - leading
    return jnp.stack([leading, trailing], axis=1).reshape(STRETCHES).astype(jnp.int32)


def set_ends(result, key, least, high):
    longest = result.shape.index(max(result.shape))
    spots = []
    for shift in (0, 1):
        where = [jax.random.randint(jax.random.fold_in(key, axis), (), 0, length) for axis, length in enumerate(result.shape)]
        where[longest] = (where[longest] + shift) % result.shape[longest]
        spots.append(tuple(where))
    return result.at[spots[0]].set(least).at[spots[1]].set(high)


def shard_levels(rng, shape, split, least, largest):
    loudness, own = 1.0, jax.random.fold_in(rng, 6)
    for position, blocks in split:
        draws = jnp.exp(jax.random.uniform(jax.random.fold_in(own, position), (blocks,), jnp.float32, least / len(split), largest / len(split)))
        loudness = loudness * jnp.repeat(draws, shape[position] // blocks).reshape([-1 if axis == position else 1 for axis in range(len(shape))])
    return loudness


def cumulative_ranks(number_of, lean):
    portions = [(1 << 20) // math.isqrt(standing ** lean) + 1 for standing in range(1, number_of + 1)]
    deviation = 1 + sum(portions) // (1 << 30)
    return np.cumsum(np.array([max(1, weight // deviation) for weight in portions]))


def ranked(own_key, extent, amount, lean):
    table = cumulative_ranks(amount, lean)
    lot = jax.random.randint(jax.random.fold_in(own_key, 1), extent, 0, int(table[amount - 1]))
    rank = jnp.searchsorted(jnp.asarray(table, jnp.int32), lot, side="right")
    return jax.random.permutation(jax.random.fold_in(own_key, 2), amount)[rank].astype(jnp.int32)


def profile(count, total, reach, skew):
    portions = [(1 << 20) // math.isqrt(grade ** skew) + 1 for grade in range(2, count + 1)]
    surplus, counts = total - reach - (count - 1), [1] * (count - 1)
    while surplus > 0:
        candidates = [i for i in range(count - 1) if counts[i] < reach]
        whole, budget = sum([portions[i] for i in candidates]), surplus
        for i in candidates:
            extra = min(reach - counts[i], max(1, budget * portions[i] // whole), surplus)
            counts[i] = counts[i] + extra
            surplus = surplus - extra
    return np.array([reach] + counts)


def ragged_sizes(rng, number_of, total, bound, skew):
    if number_of == 2:
        one = jax.random.randint(rng, (), max(1, total - bound), min(bound, total - 1) + 1)
        return jnp.stack([one, total - one])
    sizes = jnp.asarray(profile(number_of, total, bound, skew), jnp.int32)
    couples = (number_of - 1) // 2
    giver, sink = sizes[1:1 + 2 * couples:2], sizes[2:2 + 2 * couples:2]
    slack = jnp.minimum(giver - 1, bound - sink)
    moved = jax.random.randint(jax.random.fold_in(rng, 1), (couples,), 0, 1 << 20) % (slack + 1)
    sizes = sizes.at[1:1 + 2 * couples:2].set(giver - moved).at[2:2 + 2 * couples:2].set(sink + moved)
    return sizes[jax.random.permutation(jax.random.fold_in(rng, 2), number_of)]


def centred(key, extent, scale, most, split=(), kind=jnp.bfloat16):
    loudness = shard_levels(key, extent, split, -0.22, 0.18) if split else 1.0
    entries = jax.random.normal(key, extent, jnp.float32) * scale * loudness
    return jnp.minimum(jnp.maximum(entries, -most), most).astype(kind)


def setup_inputs(seed: int = 0) -> dict:
    splits = jax.random.split(jax.random.key(seed), 14)
    return {
        "hidden_in": draw_hidden_in(jax.random.fold_in(splits[13], 71), 0),
        "attn_gain": jnp.clip(1.0 + 0.18 * jax.random.normal(splits[1], (D,), jnp.float32), 0.1, 1.9),
        "w_query": draw_w_query(jax.random.fold_in(splits[13], 71), 0),
        "w_key": draw_w_key(jax.random.fold_in(splits[13], 71), 0),
        "w_value": centred(splits[4], (D, KV_HEADS * HEAD_DIM), D ** -0.5, 0.09375, ((1, 4),)),
        "w_out": centred(splits[5], (HEADS * HEAD_DIM, D), HEAD_DIM ** -0.5, 0.5, ((0, 4),)),
        "final_gain": jnp.clip(1.0 + 0.1 * jax.random.normal(splits[6], (D,), jnp.float32), 0.5, 1.5),
        "teacher_head": draw_teacher_head(jax.random.fold_in(splits[13], 71), 0),
        "draft_rows": centred(splits[8], (TOKENS, DD), 0.25, 1.5, ((0, 8),)),
        "draft_head": draw_draft_head(jax.random.fold_in(splits[13], 71), 0),
        "target_ids": set_ends(ranked(splits[10], (TOKENS,), VOCAB, 2), jax.random.fold_in(splits[10], 3), 0, VOCAB - 1).astype(jnp.int32),
        "rollout_lengths": ragged_sizes(splits[11], ROLLOUTS, TOKENS, TOKENS // 2, 2).astype(jnp.int32),
        "stretch_order": draw_stretch_order(jax.random.fold_in(splits[13], 71), 0),
    }


EPSILON = 1e-05
ROPE_BASE = 500000.0
MIXING = 0.5
NEGATIVE = -1e+30

def rms_scale(values, gain):
    mean_square = lax.optimization_barrier(jnp.mean(values * values, axis=-1, keepdims=True))
    return values * lax.rsqrt(mean_square + EPSILON) * gain

def rotate(vectors, positions):
    half_dim = vectors.shape[-1] // 2
    exponents = jnp.arange(half_dim, dtype=jnp.float32) * (2.0 / vectors.shape[-1])
    frequencies = jnp.power(ROPE_BASE, -exponents)
    angles = positions.astype(jnp.float32)[:, None] * frequencies[None, :]
    cosine_values = jnp.cos(angles)[:, None, :]
    sine_values = jnp.sin(angles)[:, None, :]
    leading = vectors[..., :half_dim]
    trailing = vectors[..., half_dim:]
    return jnp.concatenate([leading * cosine_values - trailing * sine_values, trailing * cosine_values + leading * sine_values], axis=-1)

def slab_positions(stretch_order, rollout_lengths):
    half_rows = TOK_DEV // 2
    row_ids = jnp.arange(TOKENS, dtype=jnp.int32)
    positions = (stretch_order[row_ids // half_rows] * half_rows + row_ids % half_rows).astype(jnp.int32)
    rollout_ends = jnp.cumsum(rollout_lengths).astype(jnp.int32)
    rollouts = lax.optimization_barrier(jnp.sum((positions[:, None] >= rollout_ends[None, :]).astype(jnp.int32), axis=1))
    return (positions, rollouts)

def softmax_rows(logits):
    highest = lax.optimization_barrier(jnp.max(logits, axis=1, keepdims=True))
    weights = jnp.exp(logits - highest)
    return weights / lax.optimization_barrier(jnp.sum(weights, axis=1, keepdims=True))

def row_gradients(final_rows, draft_block, target_block, teacher_head, draft_head):
    word_ids = jnp.arange(VOCAB, dtype=jnp.int32)
    teacher_logits = jnp.dot(final_rows, teacher_head.T, preferred_element_type=jnp.float32)
    draft_logits = jnp.dot(draft_block, draft_head.T, preferred_element_type=jnp.float32)
    teacher_probs = softmax_rows(teacher_logits)
    draft_probs = softmax_rows(draft_logits)
    soft = (1.0 - MIXING) * teacher_probs + jnp.where(target_block[:, None] == word_ids[None, :], MIXING, 0.0)
    delta = (draft_probs - soft).astype(jnp.bfloat16)
    return jnp.dot(delta, draft_head, preferred_element_type=jnp.float32)

def reference(hidden_in, attn_gain, w_query, w_key, w_value, w_out, final_gain, teacher_head, draft_rows, draft_head, target_ids, rollout_lengths, stretch_order):
    group_size = HEADS // KV_HEADS
    positions, rollouts = slab_positions(stretch_order, rollout_lengths)
    normed = rms_scale(hidden_in.astype(jnp.float32), attn_gain).astype(jnp.bfloat16)
    queries = jnp.dot(normed, w_query, preferred_element_type=jnp.float32).reshape(TOKENS, HEADS, HEAD_DIM)
    keys = jnp.dot(normed, w_key, preferred_element_type=jnp.float32).reshape(TOKENS, KV_HEADS, HEAD_DIM)
    values = jnp.dot(normed, w_value, preferred_element_type=jnp.float32).astype(jnp.bfloat16).reshape(TOKENS, KV_HEADS, HEAD_DIM)
    queries = rotate(queries, positions).astype(jnp.bfloat16).reshape(TOKENS, KV_HEADS, group_size, HEAD_DIM)
    keys = rotate(keys, positions).astype(jnp.bfloat16)
    allowed = (positions[None, :] <= positions[:, None]) & (rollouts[None, :] == rollouts[:, None])
    scores = jnp.einsum('qkgd,tkd->kgqt', queries.astype(jnp.float32), keys.astype(jnp.float32)) * HEAD_DIM ** (-0.5)
    scores = jnp.where(allowed[None, None], scores, NEGATIVE)
    highest = lax.optimization_barrier(jnp.max(scores, axis=-1, keepdims=True))
    expd = jnp.where(allowed[None, None], jnp.exp(scores - highest), 0.0)
    totals = lax.optimization_barrier(jnp.sum(expd, axis=-1))
    rounded = lax.optimization_barrier(expd.astype(jnp.bfloat16))
    numerators = jnp.einsum('kgqt,tkd->qkgd', rounded.astype(jnp.float32), values.astype(jnp.float32))
    attended = (numerators / jnp.transpose(totals, (2, 0, 1))[..., None]).astype(jnp.bfloat16).reshape(TOKENS, HEADS * HEAD_DIM)
    mixed = hidden_in.astype(jnp.float32) + jnp.dot(attended, w_out, preferred_element_type=jnp.float32)
    final = rms_scale(mixed, final_gain).astype(jnp.bfloat16)
    blocks = (final.reshape(N_CTX, TOK_DEV, D), draft_rows.reshape(N_CTX, TOK_DEV, DD), target_ids.reshape(N_CTX, TOK_DEV))
    grads = lax.map(lambda block: row_gradients(block[0], block[1], block[2], teacher_head, draft_head), blocks)
    return grads.reshape(TOKENS, DD)
```

```python
import functools

import jax
import jax.numpy as jnp
from jax import lax
from jax.experimental import pallas as pl
from jax.experimental.pallas import tpu as pltpu
from jax.sharding import PartitionSpec as P

HEAD_DIM = 128


EPSILON = 1e-05
ROPE_BASE = 500000.0
MIXING = 0.5
NEGATIVE = -1e30


def rms_scale(values, gain):
    mean_square = jnp.mean(values * values, axis=-1, keepdims=True)
    return values * lax.rsqrt(mean_square + EPSILON) * gain


def rotate(vectors, positions):
    half_dim = vectors.shape[-1] // 2
    exponents = jnp.arange(half_dim, dtype=jnp.float32) * (2.0 / vectors.shape[-1])
    frequencies = jnp.power(ROPE_BASE, -exponents)
    angles = positions.astype(jnp.float32)[:, None] * frequencies[None, :]
    cosine_values = jnp.cos(angles)[:, None, :]
    sine_values = jnp.sin(angles)[:, None, :]
    leading = vectors[..., :half_dim]
    trailing = vectors[..., half_dim:]
    return jnp.concatenate(
        [
            leading * cosine_values - trailing * sine_values,
            trailing * cosine_values + leading * sine_values,
        ],
        axis=-1,
    )


MESH = pl.DeviceIdType.MESH
VMEM_LIMIT = 56 * 1024 * 1024


def place():
    ctx = lax.axis_index("ctx")
    core = ctx % 2
    return ctx, lax.axis_index("vocab"), core, ctx // 2, ctx + 1 - 2 * core


def flip(index, mask):
    bit = 1
    while bit <= mask:
        if mask & bit:
            index = index + bit * (1 - 2 * ((index // bit) % 2))
        bit *= 2
    return index


def greet(devices):
    barrier = pltpu.get_barrier_semaphore()
    for device in devices:
        pl.semaphore_signal(barrier, inc=1, device_id=device, device_id_type=MESH)
    pl.semaphore_wait(barrier, len(devices))


def push(source, target, send, recv, device):
    return pltpu.make_async_remote_copy(
        src_ref=source,
        dst_ref=target,
        send_sem=send,
        recv_sem=recv,
        device_id=device,
        device_id_type=MESH,
    )


def spread(chips, peers, block, sems):
    ctx, vocab, core, chip, sibling = place()
    z_send, z_recv, v_send, v_recv, s_send, s_recv = sems
    bits = [1 << i for i in range(peers.bit_length() - 1)]
    orders = (bits, bits[::-1])
    sent = []

    def hand_on(far, mask, half):
        source = ((chip - far + chips) % chips) * 2 + core
        piece = block(source, flip(vocab, mask), half)
        reached = [i for i, bit in enumerate(orders[half]) if mask & bit]
        begin = reached[-1] + 1 if reached else 0
        for i in range(begin, len(bits)):
            bit = orders[half][i]
            sent.append(
                push(
                    piece,
                    piece,
                    v_send.at[far, half, mask, i],
                    v_recv.at[far, half, mask | bit],
                    (ctx, flip(vocab, bit)),
                )
            )
            sent[-1].start()
        sent.append(
            push(
                piece,
                piece,
                s_send.at[far, half, mask],
                s_recv.at[far, half, mask],
                (sibling, vocab),
            )
        )
        sent[-1].start()

    own = [block(ctx, vocab, half) for half in (0, 1)]
    for half in (0, 1):
        for far in range(1, chips):
            sent.append(
                push(
                    own[half],
                    own[half],
                    z_send.at[far, half],
                    z_recv.at[far, half],
                    (((chip + far) % chips) * 2 + core, vocab),
                )
            )
            sent[-1].start()
        hand_on(0, 0, half)
    for step in range(1, chips + len(bits)):
        for level in range(0, len(bits) + 1):
            far = step - level
            if not 0 <= far < chips or (far == 0 and level == 0):
                continue
            for half in (0, 1):
                for mask in [m for m in range(peers) if bin(m).count("1") == level]:
                    source = ((chip - far + chips) % chips) * 2 + core
                    piece = block(source, flip(vocab, mask), half)
                    sem = v_recv.at[far, half, mask] if mask else z_recv.at[far, half]
                    push(piece, piece, sem, sem, (sibling, vocab)).wait_recv()
                    hand_on(far, mask, half)
    for far in range(chips):
        for half in (0, 1):
            for mask in range(peers):
                source = ((chip - far + chips) % chips) * 2 + 1 - core
                piece = block(source, flip(vocab, mask), half)
                sem = s_recv.at[far, half, mask]
                push(piece, piece, sem, sem, (sibling, vocab)).wait_recv()
    for copy in sent:
        copy.wait_send()


def spread_sems(chips, peers):
    dma = pltpu.SemaphoreType.DMA
    depth = max(1, peers.bit_length() - 1)
    return [
        dma((chips, 2)),
        dma((chips, 2)),
        dma((chips, 2, peers, depth)),
        dma((chips, 2, peers)),
        dma((chips, 2, peers)),
        dma((chips, 2, peers)),
    ]


def communicate(body, out_shape, operands, scratch, collective):
    return pl.pallas_call(
        body,
        out_shape=out_shape,
        in_specs=[pl.BlockSpec(memory_space=pltpu.VMEM)] * len(operands),
        out_specs=pl.BlockSpec(memory_space=pltpu.VMEM),
        scratch_shapes=scratch,
        compiler_params=pltpu.CompilerParams(
            collective_id=collective, has_side_effects=True, vmem_limit_bytes=VMEM_LIMIT
        ),
    )(*operands)


def gather_context_body(chips, own_ref, out_ref, *sems):
    ctx, vocab, core, chip, sibling = place()
    width = own_ref.shape[1] // 2
    greet(
        [(sibling, vocab)]
        + [(((chip + far) % chips) * 2 + core, vocab) for far in range(1, chips)]
    )
    out_ref[ctx] = own_ref[...]
    spread(
        chips, 1, lambda c, v, half: out_ref.at[c, :, half * width : (half + 1) * width], sems
    )


def mix_and_gather_body(
    chips, peers, part_ref, hidden_ref, gain_ref, out_ref, send_buf, recv_buf, r_send, r_recv, *sems
):
    ctx, vocab, core, chip, sibling = place()
    width = part_ref.shape[2] // 2
    greet(
        [(sibling, vocab)]
        + [(((chip + far) % chips) * 2 + core, vocab) for far in range(1, chips)]
        + [(ctx, (vocab + far) % peers) for far in range(1, peers)]
    )
    copies = []
    for far in range(1, peers):
        owner = (vocab + far) % peers
        send_buf[far - 1] = part_ref[owner].astype(jnp.bfloat16)
        copies.append(
            push(
                send_buf.at[far - 1],
                recv_buf.at[far - 1],
                r_send.at[far - 1],
                r_recv.at[far - 1],
                (ctx, owner),
            )
        )
        copies[-1].start()
    for copy in copies:
        copy.wait_recv()
    mixed = hidden_ref[vocab].astype(jnp.float32) + part_ref[vocab]
    for far in range(1, peers):
        mixed = mixed + recv_buf[far - 1].astype(jnp.float32)
    out_ref[ctx, vocab] = rms_scale(mixed, gain_ref[...]).astype(jnp.bfloat16)
    spread(
        chips,
        peers,
        lambda c, v, half: out_ref.at[c, v, :, half * width : (half + 1) * width],
        sems,
    )
    for copy in copies:
        copy.wait_send()


def combine_pairs(former, latter):
    merged = []
    for member in (0, 2):
        highest = jnp.maximum(former[member], latter[member])
        merged += [
            highest,
            former[member + 1] * jnp.exp(former[member] - highest)
            + latter[member + 1] * jnp.exp(latter[member] - highest),
        ]
    return merged


def totals_body(chips, peers, own_ref, out_ref, held, landed, sends, recvs):
    ctx, vocab, core, chip, sibling = place()
    stages = [
        [(sibling, vocab)],
        [(ctx, (vocab + far) % peers) for far in range(1, peers)],
        [(((chip + far) % chips) * 2 + core, vocab) for far in range(1, chips)],
    ]
    greet(stages[0] + stages[1] + stages[2])
    state = [own_ref[member] for member in range(4)]
    slot, copies = 0, []
    for stage, devices in enumerate(stages):
        for member in range(4):
            held[stage, member] = state[member]
        begin = slot
        for device in devices:
            copies.append(
                push(held.at[stage], landed.at[slot], sends.at[slot], recvs.at[slot], device)
            )
            copies[-1].start()
            slot += 1
        for at in range(begin, slot):
            copies[at].wait_recv()
            state = combine_pairs(state, [landed[at, member] for member in range(4)])
    for member in range(4):
        out_ref[member] = state[member]
    for copy in copies:
        copy.wait_send()


def reduce_body(
    chips, peers, part_ref, out_ref, pair, v_src, v_dst, z_src, z_dst,
    p_send, p_recv, v_send, v_recv, z_send, z_recv,
):
    ctx, vocab, core, chip, sibling = place()
    width = part_ref.shape[2] // peers
    greet(
        [(sibling, vocab)]
        + [(((chip + far) % chips) * 2 + core, vocab) for far in range(1, chips)]
        + [(ctx, (vocab + far) % peers) for far in range(1, peers)]
    )
    pair_copies, v_copies, z_copies = [], [], []
    for step in range(chips):
        owner = (chip + step + 1) % chips
        pair_copies.append(
            push(
                part_ref.at[owner * 2 + 1 - core],
                pair.at[step],
                p_send.at[step],
                p_recv.at[step],
                (sibling, vocab),
            )
        )
        pair_copies[-1].start()

    def columns(index):
        return pl.ds(pl.multiple_of(index * width, 128), width)

    for step in range(chips):
        owner = (chip + step + 1) % chips
        pair_copies[step].wait_recv()
        for far in range(1, peers):
            target = (vocab + far) % peers
            v_src[step, far - 1] = (
                part_ref[owner * 2 + core, :, columns(target)] + pair[step, :, columns(target)]
            ).astype(jnp.bfloat16)
            v_copies.append(
                push(
                    v_src.at[step, far - 1],
                    v_dst.at[step, far - 1],
                    v_send.at[step, far - 1],
                    v_recv.at[step, far - 1],
                    (ctx, target),
                )
            )
            v_copies[-1].start()
    for step in range(chips):
        owner = (chip + step + 1) % chips
        total = part_ref[owner * 2 + core, :, columns(vocab)] + pair[step, :, columns(vocab)]
        for far in range(1, peers):
            v_copies[step * (peers - 1) + far - 1].wait_recv()
            total = total + v_dst[step, far - 1].astype(jnp.float32)
        if step < chips - 1:
            z_src[step] = total.astype(jnp.bfloat16)
            z_copies.append(
                push(
                    z_src.at[step],
                    z_dst.at[step],
                    z_send.at[step],
                    z_recv.at[step],
                    (owner * 2 + core, vocab),
                )
            )
            z_copies[-1].start()
    for step in range(chips - 1):
        z_copies[step].wait_recv()
        total = total + z_dst[step].astype(jnp.float32)
    out_ref[...] = total
    for copy in pair_copies + v_copies + z_copies:
        copy.wait_send()


def local_totals(logits):
    highest = jnp.max(logits, axis=1)
    return (highest, jnp.sum(jnp.exp(logits - highest[:, None]), axis=1))


def on_device(
    hidden_in,
    attn_gain,
    w_query,
    w_key,
    w_value,
    w_out,
    final_gain,
    teacher_head,
    draft_rows,
    draft_head,
    target_ids,
    rollout_lengths,
    stretch_order,
):
    row_count = hidden_in.shape[0]
    head_dim = HEAD_DIM
    local_heads = w_query.shape[1] // head_dim
    local_groups = w_key.shape[1] // head_dim
    group_size = local_heads // local_groups
    ctx_count = lax.axis_size("ctx")
    chips = ctx_count // 2
    peers = lax.axis_size("vocab")
    bf16, f32, dma = jnp.bfloat16, jnp.float32, pltpu.SemaphoreType.DMA
    half_rows = row_count // 2
    stretch_ids = jnp.arange(stretch_order.shape[0], dtype=jnp.int32)
    rollout_ends = jnp.cumsum(rollout_lengths)

    def locate(begin_row, span_rows):
        row_ids = begin_row + jnp.arange(span_rows, dtype=jnp.int32)
        stretch_hit = (row_ids // half_rows)[:, None] == stretch_ids[None, :]
        stretch_start = jnp.sum(jnp.where(stretch_hit, stretch_order[None, :], 0), axis=1)
        positions = stretch_start * half_rows + row_ids % half_rows
        rollouts = jnp.sum((positions[:, None] >= rollout_ends[None, :]).astype(jnp.int32), axis=1)
        return (positions, rollouts)

    query_pos, query_roll = locate(lax.axis_index("ctx") * row_count, row_count)
    normed = rms_scale(hidden_in.astype(jnp.float32), attn_gain).astype(jnp.bfloat16)
    queries = jnp.dot(normed, w_query, preferred_element_type=jnp.float32).reshape(
        row_count, local_heads, head_dim
    )
    queries = (
        rotate(queries, query_pos)
        .astype(jnp.bfloat16)
        .reshape(row_count, local_groups, group_size, head_dim)
    )
    keys = jnp.dot(normed, w_key, preferred_element_type=jnp.float32).reshape(
        row_count, local_groups, head_dim
    )
    keys = rotate(keys, query_pos).astype(jnp.bfloat16).reshape(row_count, local_groups * head_dim)
    values = jnp.dot(normed, w_value, preferred_element_type=jnp.float32).astype(jnp.bfloat16)
    score_scale = head_dim ** (-0.5)
    own = jnp.concatenate([keys, values], axis=1)
    gathered = communicate(
        functools.partial(gather_context_body, chips),
        jax.ShapeDtypeStruct((ctx_count,) + own.shape, bf16),
        (own,),
        spread_sems(chips, 1),
        0,
    ).reshape(-1, own.shape[1])
    key_piece = gathered[:, : keys.shape[1]].reshape(-1, local_groups, head_dim)
    value_piece = gathered[:, keys.shape[1] :].reshape(-1, local_groups, head_dim)
    key_count = key_piece.shape[0]
    key_pos, key_roll = locate(jnp.int32(0), key_count)
    allowed = (key_pos[None, :] <= query_pos[:, None]) & (key_roll[None, :] == query_roll[:, None])
    running_max = jnp.full((row_count, local_groups, group_size), NEGATIVE, jnp.float32)
    visible = allowed[:, None, None, :]
    scores = (
        jnp.einsum("tkgd,nkd->tkgn", queries, key_piece, preferred_element_type=jnp.float32)
        * score_scale
    )
    scores = jnp.where(visible, scores, NEGATIVE)
    new_max = jnp.maximum(running_max, jnp.max(scores, axis=-1))
    weights = jnp.where(visible, jnp.exp(scores - new_max[..., None]), 0.0)
    new_sum = jnp.sum(weights, axis=-1)
    new_weighted = jnp.einsum(
        "tkgn,nkd->tkgd",
        weights.astype(jnp.bfloat16),
        value_piece,
        preferred_element_type=jnp.float32,
    )
    attended = (
        (new_weighted / new_sum[..., None])
        .astype(jnp.bfloat16)
        .reshape(row_count, local_heads * head_dim)
    )
    partial_value = jnp.dot(attended, w_out, preferred_element_type=jnp.float32)
    width = hidden_in.shape[1]
    share = row_count // peers
    final = communicate(
        functools.partial(mix_and_gather_body, chips, peers),
        jax.ShapeDtypeStruct((ctx_count, peers, share, width), bf16),
        (
            partial_value.reshape(peers, share, width),
            hidden_in.reshape(peers, share, width),
            final_gain.reshape(1, width),
        ),
        [
            pltpu.VMEM((peers - 1, share, width), bf16),
            pltpu.VMEM((peers - 1, share, width), bf16),
            dma((peers - 1,)),
            dma((peers - 1,)),
        ]
        + spread_sems(chips, peers),
        1,
    )
    word_count = teacher_head.shape[0]
    pieces = (
        final.reshape(-1, width),
        lax.all_gather(draft_rows, "ctx", axis=0, tiled=True),
    )
    teacher_part = jnp.einsum(
        "nd,wd->nw", pieces[0], teacher_head, preferred_element_type=jnp.float32
    )
    draft_part = jnp.einsum("nd,wd->nw", pieces[1], draft_head, preferred_element_type=jnp.float32)
    teacher_max, teacher_sum = local_totals(teacher_part)
    draft_max, draft_sum = local_totals(draft_part)
    tokens = teacher_max.shape[0]
    stats = jnp.stack([teacher_max, teacher_sum, draft_max, draft_sum]).reshape(4, -1, 128)
    hops = 1 + (peers - 1) + (chips - 1)
    totals = communicate(
        functools.partial(totals_body, chips, peers),
        jax.ShapeDtypeStruct(stats.shape, f32),
        (stats,),
        [
            pltpu.VMEM((3,) + stats.shape, f32),
            pltpu.VMEM((hops,) + stats.shape, f32),
            dma((hops,)),
            dma((hops,)),
        ],
        2,
    ).reshape(4, tokens)
    teacher_probs = jnp.exp(teacher_part - totals[0][:, None]) / totals[1][:, None]
    draft_probs = jnp.exp(draft_part - totals[2][:, None]) / totals[3][:, None]
    word_start = (lax.axis_index("vocab") * ctx_count + lax.axis_index("ctx")) * word_count
    word_ids = word_start + jnp.arange(word_count, dtype=jnp.int32)
    soft = (1.0 - MIXING) * teacher_probs + jnp.where(
        target_ids[:, None] == word_ids[None, :], MIXING, 0.0
    )
    delta = (draft_probs - soft).astype(jnp.bfloat16)
    grads = jnp.dot(delta, draft_head, preferred_element_type=jnp.float32)
    features = grads.shape[1]
    slice_width = features // peers
    return communicate(
        functools.partial(reduce_body, chips, peers),
        jax.ShapeDtypeStruct((row_count, slice_width), f32),
        (grads.reshape(ctx_count, row_count, features),),
        [
            pltpu.VMEM((chips, row_count, features), f32),
            pltpu.VMEM((chips, peers - 1, row_count, slice_width), bf16),
            pltpu.VMEM((chips, peers - 1, row_count, slice_width), bf16),
            pltpu.VMEM((chips - 1, row_count, slice_width), bf16),
            pltpu.VMEM((chips - 1, row_count, slice_width), bf16),
            dma((chips,)),
            dma((chips,)),
            dma((chips, peers - 1)),
            dma((chips, peers - 1)),
            dma((chips - 1,)),
            dma((chips - 1,)),
        ],
        3,
    )


def solution(mesh):
    placed = (
        P("ctx", None),
        P(),
        P(None, "vocab"),
        P(None, "vocab"),
        P(None, "vocab"),
        P("vocab", None),
        P(),
        P(("vocab", "ctx"), None),
        P("ctx", None),
        P(("vocab", "ctx"), None),
        P(),
        P(),
        P(),
    )
    return jax.shard_map(
        on_device, mesh=mesh, in_specs=placed, out_specs=P("ctx", "vocab"), check_vma=False
    )
```

```python
import functools

import jax
import jax.numpy as jnp
from jax import lax
from jax.experimental import pallas as pl
from jax.experimental.pallas import tpu as pltpu
from jax.sharding import PartitionSpec as P

HEAD_DIM = 128


EPSILON = 1e-05
ROPE_BASE = 500000.0
MIXING = 0.5
NEGATIVE = -1e30


def rms_scale(values, gain):
    mean_square = jnp.mean(values * values, axis=-1, keepdims=True)
    return values * lax.rsqrt(mean_square + EPSILON) * gain


def rotate(vectors, positions):
    half_dim = vectors.shape[-1] // 2
    exponents = jnp.arange(half_dim, dtype=jnp.float32) * (2.0 / vectors.shape[-1])
    frequencies = jnp.power(ROPE_BASE, -exponents)
    angles = positions.astype(jnp.float32)[:, None] * frequencies[None, :]
    cosine_values = jnp.cos(angles)[:, None, :]
    sine_values = jnp.sin(angles)[:, None, :]
    leading = vectors[..., :half_dim]
    trailing = vectors[..., half_dim:]
    return jnp.concatenate(
        [
            leading * cosine_values - trailing * sine_values,
            trailing * cosine_values + leading * sine_values,
        ],
        axis=-1,
    )


MESH = pl.DeviceIdType.MESH
VMEM_LIMIT = 56 * 1024 * 1024


def place():
    ctx = lax.axis_index("ctx")
    core = ctx % 2
    return ctx, lax.axis_index("vocab"), core, ctx // 2, ctx + 1 - 2 * core


def flip(index, mask):
    bit = 1
    while bit <= mask:
        if mask & bit:
            index = index + bit * (1 - 2 * ((index // bit) % 2))
        bit *= 2
    return index


def greet(devices):
    barrier = pltpu.get_barrier_semaphore()
    for device in devices:
        pl.semaphore_signal(barrier, inc=1, device_id=device, device_id_type=MESH)
    pl.semaphore_wait(barrier, len(devices))


def push(source, target, send, recv, device):
    return pltpu.make_async_remote_copy(
        src_ref=source,
        dst_ref=target,
        send_sem=send,
        recv_sem=recv,
        device_id=device,
        device_id_type=MESH,
    )


class Spread:
    def __init__(self, chips, peers, block, sems):
        self.chips, self.peers, self.block, self.sems = chips, peers, block, sems
        self.bits = [1 << i for i in range(peers.bit_length() - 1)]
        self.orders = (self.bits, self.bits[::-1])
        self.sent = []

    def piece(self, far, mask, half, other=False):
        ctx, vocab, core, chip, sibling = place()
        source = ((chip - far + self.chips) % self.chips) * 2 + (1 - core if other else core)
        return self.block(source, flip(vocab, mask), half)

    def send(self, piece, send, recv, device):
        self.sent.append(push(piece, piece, send, recv, device))
        self.sent[-1].start()

    def arrive(self, piece, sem):
        ctx, vocab, core, chip, sibling = place()
        push(piece, piece, sem, sem, (sibling, vocab)).wait_recv()

    def hand_on(self, far, mask, half):
        ctx, vocab, core, chip, sibling = place()
        z_send, z_recv, v_send, v_recv, s_send, s_recv = self.sems
        piece = self.piece(far, mask, half)
        order = self.orders[half]
        reached = [i for i, bit in enumerate(order) if mask & bit]
        for i in range(reached[-1] + 1 if reached else 0, len(order)):
            self.send(
                piece,
                v_send.at[far, half, mask, i],
                v_recv.at[far, half, mask | order[i]],
                (ctx, flip(vocab, order[i])),
            )
        self.send(
            piece, s_send.at[far, half, mask], s_recv.at[far, half, mask], (sibling, vocab)
        )

    def start(self):
        ctx, vocab, core, chip, sibling = place()
        z_send, z_recv = self.sems[:2]
        for half in (0, 1):
            for far in range(1, self.chips):
                self.send(
                    self.piece(0, 0, half),
                    z_send.at[far, half],
                    z_recv.at[far, half],
                    (((chip + far) % self.chips) * 2 + core, vocab),
                )
            self.hand_on(0, 0, half)

    def steps(self):
        return range(1, self.chips + len(self.bits))

    def step(self, step):
        z_recv, v_recv = self.sems[1], self.sems[3]
        for level in range(0, len(self.bits) + 1):
            far = step - level
            if not 0 <= far < self.chips or (far == 0 and level == 0):
                continue
            for half in (0, 1):
                for mask in [m for m in range(self.peers) if bin(m).count("1") == level]:
                    sem = v_recv.at[far, half, mask] if mask else z_recv.at[far, half]
                    self.arrive(self.piece(far, mask, half), sem)
                    self.hand_on(far, mask, half)

    def collect(self, far):
        for half in (0, 1):
            for mask in range(self.peers):
                self.arrive(self.piece(far, mask, half, True), self.sems[5].at[far, half, mask])

    def finish(self):
        for copy in self.sent:
            copy.wait_send()


def spread_sems(chips, peers):
    dma = pltpu.SemaphoreType.DMA
    depth = max(1, peers.bit_length() - 1)
    return [
        dma((chips, 2)),
        dma((chips, 2)),
        dma((chips, 2, peers, depth)),
        dma((chips, 2, peers)),
        dma((chips, 2, peers)),
        dma((chips, 2, peers)),
    ]


def communicate(body, out_shape, operands, scratch, collective, in_kinds=None, out_kinds=None):
    in_kinds = in_kinds or [pltpu.VMEM] * len(operands)
    out_kinds = out_kinds or [pltpu.VMEM] * len(out_shape)
    return pl.pallas_call(
        body,
        out_shape=out_shape,
        in_specs=[pl.BlockSpec(memory_space=kind) for kind in in_kinds],
        out_specs=[pl.BlockSpec(memory_space=kind) for kind in out_kinds],
        scratch_shapes=scratch,
        compiler_params=pltpu.CompilerParams(
            collective_id=collective, has_side_effects=True, vmem_limit_bytes=VMEM_LIMIT
        ),
    )(*operands)


def gather_context_body(chips, own_ref, out_ref, *sems):
    ctx, vocab, core, chip, sibling = place()
    width = own_ref.shape[1] // 2
    greet(
        [(sibling, vocab)]
        + [(((chip + far) % chips) * 2 + core, vocab) for far in range(1, chips)]
    )
    out_ref[ctx] = own_ref[...]
    blocks = Spread(
        chips, 1, lambda c, v, half: out_ref.at[c, :, half * width : (half + 1) * width], sems
    )
    blocks.start()
    for step in blocks.steps():
        blocks.step(step)
    for far in range(chips):
        blocks.collect(far)
    blocks.finish()


def combine_pairs(former, latter):
    merged = []
    for member in (0, 2):
        highest = jnp.maximum(former[member], latter[member])
        merged += [
            highest,
            former[member + 1] * jnp.exp(former[member] - highest)
            + latter[member + 1] * jnp.exp(latter[member] - highest),
        ]
    return merged


def halves(rows):
    width = rows.shape[-1] // 2
    return lambda c, v, half: rows.at[c, v, :, half * width : (half + 1) * width]


def logits_body(
    chips, peers, part_ref, hidden_ref, gain_ref, draft_ref, t_head, d_head,
    t_out, d_out, totals_ref,
    final_all, draft_all, t_words, d_words, slots, columns, held, landed, send_buf, recv_buf,
    load_sem, store_sem, r_send, r_recv, x_send, x_recv, *sems,
):
    ctx, vocab, core, chip, sibling = place()
    stages = [
        [(sibling, vocab)],
        [(ctx, (vocab + far) % peers) for far in range(1, peers)],
        [(((chip + far) % chips) * 2 + core, vocab) for far in range(1, chips)],
    ]
    loads = [
        pltpu.make_async_copy(d_head, d_words, load_sem.at[0]),
        pltpu.make_async_copy(t_head, t_words, load_sem.at[1]),
    ]
    for load in loads:
        load.start()
    greet(stages[0] + stages[1] + stages[2])
    copies = []
    for far in range(1, peers):
        owner = (vocab + far) % peers
        send_buf[far - 1] = part_ref[owner].astype(jnp.bfloat16)
        copies.append(
            push(
                send_buf.at[far - 1],
                recv_buf.at[far - 1],
                r_send.at[far - 1],
                r_recv.at[far - 1],
                (ctx, owner),
            )
        )
        copies[-1].start()
    draft_all[ctx, vocab] = draft_ref[vocab]
    draft = Spread(chips, peers, halves(draft_all), sems[:6])
    teacher = Spread(chips, peers, halves(final_all), sems[6:])
    draft.start()
    for step in range(1, chips):
        draft.step(step)
    for copy in copies:
        copy.wait_recv()
    mixed = hidden_ref[vocab].astype(jnp.float32) + part_ref[vocab]
    for far in range(1, peers):
        mixed = mixed + recv_buf[far - 1].astype(jnp.float32)
    final_all[ctx, vocab] = rms_scale(mixed, gain_ref[...]).astype(jnp.bfloat16)
    teacher.start()
    for step in draft.steps():
        if step >= chips:
            draft.step(step)

    rows, words = slots.shape[1], slots.shape[2]
    tile = min(words, 512)
    group = 32
    held[...] = jnp.zeros_like(held)
    stores = []

    def multiply(blocks, source_ref, head_ref, out_ref, member, far):
        count = len(stores)
        slot = count % 2
        blocks.collect(far)
        owner = (chip - far + chips) % chips
        if count >= 2:
            stores[count - 2].wait()

        def over_words(i, carry):
            at = pl.ds(pl.multiple_of(i * tile, tile), tile)
            left = source_ref[pl.ds(owner * 2, 2)].reshape(rows, source_ref.shape[3])
            slots[slot, :, at] = lax.dot_general(
                left,
                head_ref[at, :],
                (((1,), (1,)), ((), ())),
                preferred_element_type=jnp.float32,
            )
            return carry

        lax.fori_loop(0, words // tile, over_words, 0)
        store = pltpu.make_async_copy(
            slots.at[slot],
            out_ref.at[pl.ds(pl.multiple_of(owner * rows, rows), rows)],
            store_sem.at[count],
        )
        store.start()
        stores.append(store)

        def over_rows(i, carry):
            at = pl.ds(pl.multiple_of(i * group, group), group)
            values = slots[slot, at, :]
            highest = jnp.max(values, axis=1, keepdims=True)
            summed = jnp.sum(jnp.exp(values - highest), axis=1, keepdims=True)
            columns[0, at, :] = jnp.broadcast_to(highest, (group, 128))
            columns[1, at, :] = jnp.broadcast_to(summed, (group, 128))
            return carry

        lax.fori_loop(0, rows // group, over_rows, 0)
        lanes = pl.ds(pl.multiple_of(owner * rows, rows), rows)
        for which in (0, 1):
            held[0, member + which : member + which + 1, lanes] = jnp.transpose(columns[which])[:1]

    for load in loads:
        load.wait()
    done = [0, 0]
    for step in teacher.steps():
        teacher.step(step)
        if done[0] < chips:
            multiply(draft, draft_all, d_words, d_out, 2, done[0])
            done[0] += 1
        if step > len(teacher.bits):
            multiply(teacher, final_all, t_words, t_out, 0, done[1])
            done[1] += 1
    for far in range(done[0], chips):
        multiply(draft, draft_all, d_words, d_out, 2, far)
    for far in range(done[1], chips):
        multiply(teacher, final_all, t_words, t_out, 0, far)

    state = [held[0, member : member + 1] for member in range(4)]
    slot, x_copies = 0, []
    for stage, devices in enumerate(stages):
        if stage:
            for member in range(4):
                held[stage, member : member + 1] = state[member]
        begin = slot
        for device in devices:
            x_copies.append(
                push(held.at[stage], landed.at[slot], x_send.at[slot], x_recv.at[slot], device)
            )
            x_copies[-1].start()
            slot += 1
        for at in range(begin, slot):
            x_copies[at].wait_recv()
            state = combine_pairs(
                state, [landed[at, member : member + 1] for member in range(4)]
            )
    totals_ref[...] = jnp.zeros_like(totals_ref)
    for member in range(4):
        totals_ref[member : member + 1] = state[member]
    for copy in copies + x_copies:
        copy.wait_send()
    draft.finish()
    teacher.finish()
    for store in stores[-2:]:
        store.wait()


def gradient_body(
    chips, peers, totals_ref, target_ref, t_logits, d_logits, d_head, out_ref,
    d_words, t_rows, d_rows, delta, grads, pair, v_src, v_dst, z_src, z_dst,
    load_sem, t_sem, d_sem, p_send, p_recv, v_send, v_recv, z_send, z_recv,
):
    ctx, vocab, core, chip, sibling = place()
    rows, words = t_rows.shape[1], t_rows.shape[2]
    half_rows = rows // 2
    width = out_ref.shape[1]
    features = d_words.shape[1]
    tile = min(features, 512)
    group = 32
    word_start = (vocab * chips * 2 + ctx) * words

    def block_rows(step):
        owner = (chip + step + 1) % chips
        return pl.ds(pl.multiple_of(owner * rows, rows), rows)

    def fetch(step):
        slot = step % 2
        pairs = [
            pltpu.make_async_copy(
                t_logits.at[block_rows(step)], t_rows.at[slot], t_sem.at[step]
            ),
            pltpu.make_async_copy(
                d_logits.at[block_rows(step)], d_rows.at[slot], d_sem.at[step]
            ),
        ]
        for item in pairs:
            item.start()
        return pairs

    fetched = [fetch(0)]
    load = pltpu.make_async_copy(d_head, d_words, load_sem.at[0])
    load.start()
    greet(
        [(sibling, vocab)]
        + [(((chip + far) % chips) * 2 + core, vocab) for far in range(1, chips)]
        + [(ctx, (vocab + far) % peers) for far in range(1, peers)]
    )
    pair_copies, v_copies, z_copies = [], {}, []

    def column(values):
        return jnp.transpose(jnp.broadcast_to(values, (128, rows)))[:, :1]

    def features_of(index):
        return pl.ds(pl.multiple_of(index * width, 128), width)

    def make(step):
        slot = step % 2
        for item in fetched[step]:
            item.wait()
        if step + 1 < chips:
            fetched.append(fetch(step + 1))
        lanes = block_rows(step)
        t_high = column(totals_ref[0:1, lanes])
        t_scale = column((1.0 - MIXING) / totals_ref[1:2, lanes])
        d_high = column(totals_ref[2:3, lanes])
        d_scale = column(1.0 / totals_ref[3:4, lanes])
        target = column(target_ref[0:1, lanes]).astype(jnp.int32)
        ids = word_start + lax.broadcasted_iota(jnp.int32, (group, words), 1)
        for begin in range(0, rows, group):
            at = slice(begin, begin + group)
            soft = jnp.exp(t_rows[slot, at, :] - t_high[at]) * t_scale[at] + jnp.where(
                target[at] == ids, MIXING, 0.0
            )
            drafted = jnp.exp(d_rows[slot, at, :] - d_high[at]) * d_scale[at]
            delta[at, :] = (drafted - soft).astype(jnp.bfloat16)
        if step == 0:
            load.wait()

        def over_features(i, carry):
            at = pl.ds(pl.multiple_of(i * tile, tile), tile)
            product = jnp.dot(delta[...], d_words[:, at], preferred_element_type=jnp.float32)
            grads[step, 0, :, at] = product[:half_rows]
            grads[step, 1, :, at] = product[half_rows:]
            return carry

        lax.fori_loop(0, features // tile, over_features, 0)
        pair_copies.append(
            push(
                grads.at[step, 1 - core],
                pair.at[step],
                p_send.at[step],
                p_recv.at[step],
                (sibling, vocab),
            )
        )
        pair_copies[-1].start()

    def over_vocab(step):
        pair_copies[step].wait_recv()
        for far in range(1, peers):
            at = features_of((vocab + far) % peers)
            v_src[step, far - 1] = (grads[step, core, :, at] + pair[step, :, at]).astype(
                jnp.bfloat16
            )
            v_copies[step, far] = push(
                v_src.at[step, far - 1],
                v_dst.at[step, far - 1],
                v_send.at[step, far - 1],
                v_recv.at[step, far - 1],
                (ctx, (vocab + far) % peers),
            )
            v_copies[step, far].start()

    def over_chips(step):
        at = features_of(vocab)
        total = grads[step, core, :, at] + pair[step, :, at]
        for far in range(1, peers):
            v_copies[step, far].wait_recv()
            total = total + v_dst[step, far - 1].astype(jnp.float32)
        if step == chips - 1:
            return total
        z_src[step] = total.astype(jnp.bfloat16)
        owner = (chip + step + 1) % chips
        z_copies.append(
            push(
                z_src.at[step],
                z_dst.at[step],
                z_send.at[step],
                z_recv.at[step],
                (owner * 2 + core, vocab),
            )
        )
        z_copies[-1].start()
        return total

    for step in range(chips + 2):
        if step < chips:
            make(step)
        if 0 <= step - 1 < chips:
            over_vocab(step - 1)
        if 0 <= step - 2 < chips:
            total = over_chips(step - 2)
    for step in range(chips - 1):
        z_copies[step].wait_recv()
        total = total + z_dst[step].astype(jnp.float32)
    out_ref[...] = total
    for copy in pair_copies + list(v_copies.values()) + z_copies:
        copy.wait_send()


def on_device(
    hidden_in,
    attn_gain,
    w_query,
    w_key,
    w_value,
    w_out,
    final_gain,
    teacher_head,
    draft_rows,
    draft_head,
    target_ids,
    rollout_lengths,
    stretch_order,
):
    row_count = hidden_in.shape[0]
    head_dim = HEAD_DIM
    local_heads = w_query.shape[1] // head_dim
    local_groups = w_key.shape[1] // head_dim
    group_size = local_heads // local_groups
    ctx_count = lax.axis_size("ctx")
    chips = ctx_count // 2
    peers = lax.axis_size("vocab")
    bf16, f32, dma = jnp.bfloat16, jnp.float32, pltpu.SemaphoreType.DMA
    half_rows = row_count // 2
    stretch_ids = jnp.arange(stretch_order.shape[0], dtype=jnp.int32)
    rollout_ends = jnp.cumsum(rollout_lengths)

    def locate(begin_row, span_rows):
        row_ids = begin_row + jnp.arange(span_rows, dtype=jnp.int32)
        stretch_hit = (row_ids // half_rows)[:, None] == stretch_ids[None, :]
        stretch_start = jnp.sum(jnp.where(stretch_hit, stretch_order[None, :], 0), axis=1)
        positions = stretch_start * half_rows + row_ids % half_rows
        rollouts = jnp.sum((positions[:, None] >= rollout_ends[None, :]).astype(jnp.int32), axis=1)
        return (positions, rollouts)

    query_pos, query_roll = locate(lax.axis_index("ctx") * row_count, row_count)
    normed = rms_scale(hidden_in.astype(jnp.float32), attn_gain).astype(jnp.bfloat16)
    queries = jnp.dot(normed, w_query, preferred_element_type=jnp.float32).reshape(
        row_count, local_heads, head_dim
    )
    queries = (
        rotate(queries, query_pos)
        .astype(jnp.bfloat16)
        .reshape(row_count, local_groups, group_size, head_dim)
    )
    keys = jnp.dot(normed, w_key, preferred_element_type=jnp.float32).reshape(
        row_count, local_groups, head_dim
    )
    keys = rotate(keys, query_pos).astype(jnp.bfloat16).reshape(row_count, local_groups * head_dim)
    values = jnp.dot(normed, w_value, preferred_element_type=jnp.float32).astype(jnp.bfloat16)
    score_scale = head_dim ** (-0.5)
    own = jnp.concatenate([keys, values], axis=1)
    gathered = communicate(
        functools.partial(gather_context_body, chips),
        [jax.ShapeDtypeStruct((ctx_count,) + own.shape, bf16)],
        (own,),
        spread_sems(chips, 1),
        0,
    )[0].reshape(-1, own.shape[1])
    key_piece = gathered[:, : keys.shape[1]].reshape(-1, local_groups, head_dim)
    value_piece = gathered[:, keys.shape[1] :].reshape(-1, local_groups, head_dim)
    key_count = key_piece.shape[0]
    key_pos, key_roll = locate(jnp.int32(0), key_count)
    allowed = (key_pos[None, :] <= query_pos[:, None]) & (key_roll[None, :] == query_roll[:, None])
    running_max = jnp.full((row_count, local_groups, group_size), NEGATIVE, jnp.float32)
    visible = allowed[:, None, None, :]
    scores = (
        jnp.einsum("tkgd,nkd->tkgn", queries, key_piece, preferred_element_type=jnp.float32)
        * score_scale
    )
    scores = jnp.where(visible, scores, NEGATIVE)
    new_max = jnp.maximum(running_max, jnp.max(scores, axis=-1))
    weights = jnp.where(visible, jnp.exp(scores - new_max[..., None]), 0.0)
    new_sum = jnp.sum(weights, axis=-1)
    new_weighted = jnp.einsum(
        "tkgn,nkd->tkgd",
        weights.astype(jnp.bfloat16),
        value_piece,
        preferred_element_type=jnp.float32,
    )
    attended = (
        (new_weighted / new_sum[..., None])
        .astype(jnp.bfloat16)
        .reshape(row_count, local_heads * head_dim)
    )
    partial_value = jnp.dot(attended, w_out, preferred_element_type=jnp.float32)
    width = hidden_in.shape[1]
    share = row_count // peers
    word_count, features = draft_head.shape
    tokens = row_count * ctx_count
    unit = 2 * row_count
    hops = 1 + (peers - 1) + (chips - 1)
    logits = jax.ShapeDtypeStruct((tokens, word_count), f32)
    teacher_part, draft_part, totals = communicate(
        functools.partial(logits_body, chips, peers),
        [logits, logits, jax.ShapeDtypeStruct((8, tokens), f32)],
        (
            partial_value.reshape(peers, share, width),
            hidden_in.reshape(peers, share, width),
            final_gain.reshape(1, width),
            draft_rows.reshape(peers, share, features),
            teacher_head,
            draft_head,
        ),
        [
            pltpu.VMEM((ctx_count, peers, share, width), bf16),
            pltpu.VMEM((ctx_count, peers, share, features), bf16),
            pltpu.VMEM(teacher_head.shape, bf16),
            pltpu.VMEM(draft_head.shape, bf16),
            pltpu.VMEM((2, unit, word_count), f32),
            pltpu.VMEM((2, unit, 128), f32),
            pltpu.VMEM((3, 8, tokens), f32),
            pltpu.VMEM((hops, 8, tokens), f32),
            pltpu.VMEM((peers - 1, share, width), bf16),
            pltpu.VMEM((peers - 1, share, width), bf16),
            dma((2,)),
            dma((2 * chips,)),
            dma((peers - 1,)),
            dma((peers - 1,)),
            dma((hops,)),
            dma((hops,)),
        ]
        + spread_sems(chips, peers)
        + spread_sems(chips, peers),
        1,
        [pltpu.VMEM] * 4 + [pl.ANY] * 2,
        [pl.ANY, pl.ANY, pltpu.VMEM],
    )
    slice_width = features // peers
    return communicate(
        functools.partial(gradient_body, chips, peers),
        [jax.ShapeDtypeStruct((row_count, slice_width), f32)],
        (
            totals,
            target_ids.astype(f32).reshape(1, tokens),
            teacher_part,
            draft_part,
            draft_head,
        ),
        [
            pltpu.VMEM(draft_head.shape, bf16),
            pltpu.VMEM((2, unit, word_count), f32),
            pltpu.VMEM((2, unit, word_count), f32),
            pltpu.VMEM((unit, word_count), bf16),
            pltpu.VMEM((chips, 2, row_count, features), f32),
            pltpu.VMEM((chips, row_count, features), f32),
            pltpu.VMEM((chips, peers - 1, row_count, slice_width), bf16),
            pltpu.VMEM((chips, peers - 1, row_count, slice_width), bf16),
            pltpu.VMEM((chips - 1, row_count, slice_width), bf16),
            pltpu.VMEM((chips - 1, row_count, slice_width), bf16),
            dma((1,)),
            dma((chips,)),
            dma((chips,)),
            dma((chips,)),
            dma((chips,)),
            dma((chips, peers - 1)),
            dma((chips, peers - 1)),
            dma((chips - 1,)),
            dma((chips - 1,)),
        ],
        2,
        [pltpu.VMEM] * 2 + [pl.ANY] * 3,
    )[0]


def solution(mesh):
    placed = (
        P("ctx", None),
        P(),
        P(None, "vocab"),
        P(None, "vocab"),
        P(None, "vocab"),
        P("vocab", None),
        P(),
        P(("vocab", "ctx"), None),
        P("ctx", None),
        P(("vocab", "ctx"), None),
        P(),
        P(),
        P(),
    )
    return jax.shard_map(
        on_device, mesh=mesh, in_specs=placed, out_specs=P("ctx", "vocab"), check_vma=False
    )
```

```python
import functools

import jax
import jax.numpy as jnp
from jax import lax
from jax.experimental import pallas as pl
from jax.experimental.pallas import tpu as pltpu
from jax.sharding import PartitionSpec as P

HEAD_DIM = 128


EPSILON = 1e-05
ROPE_BASE = 500000.0
MIXING = 0.5
NEGATIVE = -1e30


def rms_scale(values, gain):
    mean_square = jnp.mean(values * values, axis=-1, keepdims=True)
    return values * lax.rsqrt(mean_square + EPSILON) * gain


def rotate(vectors, positions):
    half_dim = vectors.shape[-1] // 2
    exponents = jnp.arange(half_dim, dtype=jnp.float32) * (2.0 / vectors.shape[-1])
    frequencies = jnp.power(ROPE_BASE, -exponents)
    angles = positions.astype(jnp.float32)[:, None] * frequencies[None, :]
    cosine_values = jnp.cos(angles)[:, None, :]
    sine_values = jnp.sin(angles)[:, None, :]
    leading = vectors[..., :half_dim]
    trailing = vectors[..., half_dim:]
    return jnp.concatenate(
        [
            leading * cosine_values - trailing * sine_values,
            trailing * cosine_values + leading * sine_values,
        ],
        axis=-1,
    )


MESH = pl.DeviceIdType.MESH
VMEM_LIMIT = 56 * 1024 * 1024


def place():
    ctx = lax.axis_index("ctx")
    core = ctx % 2
    return ctx, lax.axis_index("vocab"), core, ctx // 2, ctx + 1 - 2 * core


def flip(index, mask):
    bit = 1
    while bit <= mask:
        if mask & bit:
            index = index + bit * (1 - 2 * ((index // bit) % 2))
        bit *= 2
    return index


def greet(devices):
    barrier = pltpu.get_barrier_semaphore()
    for device in devices:
        pl.semaphore_signal(barrier, inc=1, device_id=device, device_id_type=MESH)
    pl.semaphore_wait(barrier, len(devices))


def push(source, target, send, recv, device):
    return pltpu.make_async_remote_copy(
        src_ref=source,
        dst_ref=target,
        send_sem=send,
        recv_sem=recv,
        device_id=device,
        device_id_type=MESH,
    )


class Spread:
    def __init__(self, chips, peers, block, sems):
        self.chips, self.peers, self.block, self.sems = chips, peers, block, sems
        self.bits = [1 << i for i in range(peers.bit_length() - 1)]
        self.orders = (self.bits, self.bits[::-1])
        self.sent = []

    def piece(self, far, mask, half, other=False):
        ctx, vocab, core, chip, sibling = place()
        source = ((chip - far + self.chips) % self.chips) * 2 + (1 - core if other else core)
        return self.block(source, flip(vocab, mask), half)

    def send(self, piece, send, recv, device):
        self.sent.append(push(piece, piece, send, recv, device))
        self.sent[-1].start()

    def arrive(self, piece, sem):
        ctx, vocab, core, chip, sibling = place()
        push(piece, piece, sem, sem, (sibling, vocab)).wait_recv()

    def hand_on(self, far, mask, half):
        ctx, vocab, core, chip, sibling = place()
        z_send, z_recv, v_send, v_recv, s_send, s_recv = self.sems
        piece = self.piece(far, mask, half)
        order = self.orders[half]
        reached = [i for i, bit in enumerate(order) if mask & bit]
        for i in range(reached[-1] + 1 if reached else 0, len(order)):
            self.send(
                piece,
                v_send.at[far, half, mask, i],
                v_recv.at[far, half, mask | order[i]],
                (ctx, flip(vocab, order[i])),
            )
        self.send(
            piece, s_send.at[far, half, mask], s_recv.at[far, half, mask], (sibling, vocab)
        )

    def start(self):
        ctx, vocab, core, chip, sibling = place()
        z_send, z_recv = self.sems[:2]
        for half in (0, 1):
            for far in range(1, self.chips):
                self.send(
                    self.piece(0, 0, half),
                    z_send.at[far, half],
                    z_recv.at[far, half],
                    (((chip + far) % self.chips) * 2 + core, vocab),
                )
            self.hand_on(0, 0, half)

    def steps(self):
        return range(1, self.chips + len(self.bits))

    def step(self, step):
        z_recv, v_recv = self.sems[1], self.sems[3]
        for level in range(0, len(self.bits) + 1):
            far = step - level
            if not 0 <= far < self.chips or (far == 0 and level == 0):
                continue
            for half in (0, 1):
                for mask in [m for m in range(self.peers) if bin(m).count("1") == level]:
                    sem = v_recv.at[far, half, mask] if mask else z_recv.at[far, half]
                    self.arrive(self.piece(far, mask, half), sem)
                    self.hand_on(far, mask, half)

    def collect(self, far):
        for half in (0, 1):
            for mask in range(self.peers):
                self.arrive(self.piece(far, mask, half, True), self.sems[5].at[far, half, mask])

    def finish(self):
        for copy in self.sent:
            copy.wait_send()


def spread_sems(chips, peers):
    dma = pltpu.SemaphoreType.DMA
    depth = max(1, peers.bit_length() - 1)
    return [
        dma((chips, 2)),
        dma((chips, 2)),
        dma((chips, 2, peers, depth)),
        dma((chips, 2, peers)),
        dma((chips, 2, peers)),
        dma((chips, 2, peers)),
    ]


def communicate(body, out_shape, operands, scratch, collective, in_kinds=None, out_kinds=None):
    in_kinds = in_kinds or [pltpu.VMEM] * len(operands)
    out_kinds = out_kinds or [pltpu.VMEM] * len(out_shape)
    return pl.pallas_call(
        body,
        out_shape=out_shape,
        in_specs=[pl.BlockSpec(memory_space=kind) for kind in in_kinds],
        out_specs=[pl.BlockSpec(memory_space=kind) for kind in out_kinds],
        scratch_shapes=scratch,
        compiler_params=pltpu.CompilerParams(
            collective_id=collective, has_side_effects=True, vmem_limit_bytes=VMEM_LIMIT
        ),
    )(*operands)


def halves(rows):
    width = rows.shape[-1] // 2
    return lambda c, v, half: rows.at[c, v, :, half * width : (half + 1) * width]


def context_body(
    chips, peers, own_ref, query_ref, q_pos, q_roll, k_pos, k_roll, draft_ref,
    attended_ref, draft_all, context, mask, *sems,
):
    ctx, vocab, core, chip, sibling = place()
    half_width = own_ref.shape[1] // 2
    tokens = mask.shape[1]
    heads = query_ref.shape[1] // HEAD_DIM
    group_size = heads // (half_width // HEAD_DIM)
    greet(
        [(sibling, vocab)]
        + [(((chip + far) % chips) * 2 + core, vocab) for far in range(1, chips)]
        + [(ctx, (vocab + far) % peers) for far in range(1, peers)]
    )
    context[ctx] = own_ref[...]
    blocks = Spread(
        chips,
        1,
        lambda c, v, half: context.at[c, :, half * half_width : (half + 1) * half_width],
        sems[:6],
    )
    blocks.start()
    draft_all[ctx, vocab] = draft_ref[vocab]
    draft = Spread(chips, peers, halves(draft_all), sems[6:])
    draft.start()
    allowed = (k_pos[...] <= q_pos[...]) & (k_roll[...] == q_roll[...])
    mask[...] = jnp.where(allowed, 1.0, 0.0)
    for step in blocks.steps():
        blocks.step(step)
    pending = list(draft.steps())
    for step in pending[: chips - 1]:
        draft.step(step)
    pending = pending[chips - 1 :]
    for far in range(chips):
        blocks.collect(far)
    for head in range(heads):
        at = slice(head * HEAD_DIM, (head + 1) * HEAD_DIM)
        begin = (head // group_size) * HEAD_DIM
        keys = context[:, :, begin : begin + HEAD_DIM].reshape(tokens, HEAD_DIM)
        values = context[:, :, half_width + begin : half_width + begin + HEAD_DIM].reshape(
            tokens, HEAD_DIM
        )
        scores = lax.dot_general(
            query_ref[:, at],
            keys,
            (((1,), (1,)), ((), ())),
            preferred_element_type=jnp.float32,
        ) * (HEAD_DIM ** (-0.5))
        scores = jnp.where(mask[...] > 0.0, scores, NEGATIVE)
        weights = jnp.exp(scores - jnp.max(scores, axis=1, keepdims=True))
        weighted = jnp.dot(
            weights.astype(jnp.bfloat16), values, preferred_element_type=jnp.float32
        )
        attended_ref[:, at] = (weighted / jnp.sum(weights, axis=1, keepdims=True)).astype(
            jnp.bfloat16
        )
        if pending and head % 2 == 1:
            draft.step(pending.pop(0))
    for step in pending:
        draft.step(step)
    for far in range(chips):
        draft.collect(far)
    blocks.finish()
    draft.finish()


def combine_pairs(former, latter):
    merged = []
    for member in (0, 2):
        highest = jnp.maximum(former[member], latter[member])
        merged += [
            highest,
            former[member + 1] * jnp.exp(former[member] - highest)
            + latter[member + 1] * jnp.exp(latter[member] - highest),
        ]
    return merged


def logits_body(
    chips, peers, part_ref, hidden_ref, gain_ref, draft_from, t_head, d_head,
    t_out, d_out, totals_ref,
    final_all, draft_all, t_words, d_words, slots, columns, held, landed, send_buf, recv_buf,
    load_sem, store_sem, r_send, r_recv, x_send, x_recv, *sems,
):
    ctx, vocab, core, chip, sibling = place()
    stages = [
        [(sibling, vocab)],
        [(ctx, (vocab + far) % peers) for far in range(1, peers)],
        [(((chip + far) % chips) * 2 + core, vocab) for far in range(1, chips)],
    ]
    loads = [
        pltpu.make_async_copy(d_head, d_words, load_sem.at[0]),
        pltpu.make_async_copy(draft_from, draft_all, load_sem.at[1]),
        pltpu.make_async_copy(t_head, t_words, load_sem.at[2]),
    ]
    for load in loads:
        load.start()
    greet(stages[0] + stages[1] + stages[2])
    copies = []
    for far in range(1, peers):
        owner = (vocab + far) % peers
        send_buf[far - 1] = part_ref[owner].astype(jnp.bfloat16)
        copies.append(
            push(
                send_buf.at[far - 1],
                recv_buf.at[far - 1],
                r_send.at[far - 1],
                r_recv.at[far - 1],
                (ctx, owner),
            )
        )
        copies[-1].start()
    teacher = Spread(chips, peers, halves(final_all), sems)

    rows, words = slots.shape[1], slots.shape[2]
    tile = min(words, 512)
    group = 32
    held[...] = jnp.zeros_like(held)
    stores = []

    def multiply(blocks, source_ref, head_ref, out_ref, member, far):
        count = len(stores)
        slot = count % 2
        if blocks is not None:
            blocks.collect(far)
        owner = (chip - far + chips) % chips
        if count >= 2:
            stores[count - 2].wait()

        def over_words(i, carry):
            at = pl.ds(pl.multiple_of(i * tile, tile), tile)
            left = source_ref[pl.ds(owner * 2, 2)].reshape(rows, source_ref.shape[3])
            slots[slot, :, at] = lax.dot_general(
                left,
                head_ref[at, :],
                (((1,), (1,)), ((), ())),
                preferred_element_type=jnp.float32,
            )
            return carry

        lax.fori_loop(0, words // tile, over_words, 0)
        store = pltpu.make_async_copy(
            slots.at[slot],
            out_ref.at[pl.ds(pl.multiple_of(owner * rows, rows), rows)],
            store_sem.at[count],
        )
        store.start()
        stores.append(store)

        def over_rows(i, carry):
            at = pl.ds(pl.multiple_of(i * group, group), group)
            values = slots[slot, at, :]
            highest = jnp.max(values, axis=1, keepdims=True)
            summed = jnp.sum(jnp.exp(values - highest), axis=1, keepdims=True)
            columns[0, at, :] = jnp.broadcast_to(highest, (group, 128))
            columns[1, at, :] = jnp.broadcast_to(summed, (group, 128))
            return carry

        lax.fori_loop(0, rows // group, over_rows, 0)
        lanes = pl.ds(pl.multiple_of(owner * rows, rows), rows)
        for which in (0, 1):
            held[0, member + which : member + which + 1, lanes] = jnp.transpose(columns[which])[:1]

    def draft_unit(far):
        multiply(None, draft_all, d_words, d_out, 2, far)

    def teacher_unit(far):
        multiply(teacher, final_all, t_words, t_out, 0, far)

    loads[0].wait()
    loads[1].wait()
    early = (chips + 1) // 2
    for far in range(early):
        draft_unit(far)
    for copy in copies:
        copy.wait_recv()
    mixed = hidden_ref[vocab].astype(jnp.float32) + part_ref[vocab]
    for far in range(1, peers):
        mixed = mixed + recv_buf[far - 1].astype(jnp.float32)
    final_all[ctx, vocab] = rms_scale(mixed, gain_ref[...]).astype(jnp.bfloat16)
    teacher.start()
    loads[2].wait()
    waiting = list(range(early, chips))
    done = 0
    for step in teacher.steps():
        teacher.step(step)
        if waiting:
            draft_unit(waiting.pop(0))
        if step > len(teacher.bits):
            teacher_unit(done)
            done += 1
    for far in waiting:
        draft_unit(far)
    for far in range(done, chips):
        teacher_unit(far)

    state = [held[0, member : member + 1] for member in range(4)]
    slot, x_copies = 0, []
    for stage, devices in enumerate(stages):
        if stage:
            for member in range(4):
                held[stage, member : member + 1] = state[member]
        begin = slot
        for device in devices:
            x_copies.append(
                push(held.at[stage], landed.at[slot], x_send.at[slot], x_recv.at[slot], device)
            )
            x_copies[-1].start()
            slot += 1
        for at in range(begin, slot):
            x_copies[at].wait_recv()
            state = combine_pairs(
                state, [landed[at, member : member + 1] for member in range(4)]
            )
    totals_ref[...] = jnp.zeros_like(totals_ref)
    for member in range(4):
        totals_ref[member : member + 1] = state[member]
    for copy in copies + x_copies:
        copy.wait_send()
    teacher.finish()
    for store in stores[-2:]:
        store.wait()


def gradient_body(
    chips, peers, totals_ref, target_ref, t_logits, d_logits, d_head, out_ref,
    d_words, t_rows, d_rows, delta, grads, pair, v_src, v_dst, z_src, z_dst,
    load_sem, t_sem, d_sem, p_send, p_recv, v_send, v_recv, z_send, z_recv,
):
    ctx, vocab, core, chip, sibling = place()
    rows, words = t_rows.shape[1], t_rows.shape[2]
    half_rows = rows // 2
    width = out_ref.shape[1]
    features = d_words.shape[1]
    tile = min(features, 512)
    group = 32
    word_start = (vocab * chips * 2 + ctx) * words

    def block_rows(step):
        owner = (chip + step + 1) % chips
        return pl.ds(pl.multiple_of(owner * rows, rows), rows)

    def fetch(step):
        slot = step % 2
        pairs = [
            pltpu.make_async_copy(
                t_logits.at[block_rows(step)], t_rows.at[slot], t_sem.at[step]
            ),
            pltpu.make_async_copy(
                d_logits.at[block_rows(step)], d_rows.at[slot], d_sem.at[step]
            ),
        ]
        for item in pairs:
            item.start()
        return pairs

    fetched = [fetch(0)]
    load = pltpu.make_async_copy(d_head, d_words, load_sem.at[0])
    load.start()
    greet(
        [(sibling, vocab)]
        + [(((chip + far) % chips) * 2 + core, vocab) for far in range(1, chips)]
        + [(ctx, (vocab + far) % peers) for far in range(1, peers)]
    )
    pair_copies, v_copies, z_copies = [], {}, []

    def column(values):
        return jnp.transpose(jnp.broadcast_to(values, (128, rows)))[:, :1]

    def features_of(index):
        return pl.ds(pl.multiple_of(index * width, 128), width)

    def make(step):
        slot = step % 2
        for item in fetched[step]:
            item.wait()
        if step + 1 < chips:
            fetched.append(fetch(step + 1))
        lanes = block_rows(step)
        t_high = column(totals_ref[0:1, lanes])
        t_scale = column((1.0 - MIXING) / totals_ref[1:2, lanes])
        d_high = column(totals_ref[2:3, lanes])
        d_scale = column(1.0 / totals_ref[3:4, lanes])
        target = column(target_ref[0:1, lanes]).astype(jnp.int32)
        ids = word_start + lax.broadcasted_iota(jnp.int32, (group, words), 1)
        for begin in range(0, rows, group):
            at = slice(begin, begin + group)
            soft = jnp.exp(t_rows[slot, at, :] - t_high[at]) * t_scale[at] + jnp.where(
                target[at] == ids, MIXING, 0.0
            )
            drafted = jnp.exp(d_rows[slot, at, :] - d_high[at]) * d_scale[at]
            delta[at, :] = (drafted - soft).astype(jnp.bfloat16)
        if step == 0:
            load.wait()

        def over_features(i, carry):
            at = pl.ds(pl.multiple_of(i * tile, tile), tile)
            product = jnp.dot(delta[...], d_words[:, at], preferred_element_type=jnp.float32)
            grads[step, 0, :, at] = product[:half_rows]
            grads[step, 1, :, at] = product[half_rows:]
            return carry

        lax.fori_loop(0, features // tile, over_features, 0)
        pair_copies.append(
            push(
                grads.at[step, 1 - core],
                pair.at[step],
                p_send.at[step],
                p_recv.at[step],
                (sibling, vocab),
            )
        )
        pair_copies[-1].start()

    def over_vocab(step):
        pair_copies[step].wait_recv()
        for far in range(1, peers):
            at = features_of((vocab + far) % peers)
            v_src[step, far - 1] = (grads[step, core, :, at] + pair[step, :, at]).astype(
                jnp.bfloat16
            )
            v_copies[step, far] = push(
                v_src.at[step, far - 1],
                v_dst.at[step, far - 1],
                v_send.at[step, far - 1],
                v_recv.at[step, far - 1],
                (ctx, (vocab + far) % peers),
            )
            v_copies[step, far].start()

    def over_chips(step):
        at = features_of(vocab)
        total = grads[step, core, :, at] + pair[step, :, at]
        for far in range(1, peers):
            v_copies[step, far].wait_recv()
            total = total + v_dst[step, far - 1].astype(jnp.float32)
        if step == chips - 1:
            return total
        z_src[step] = total.astype(jnp.bfloat16)
        owner = (chip + step + 1) % chips
        z_copies.append(
            push(
                z_src.at[step],
                z_dst.at[step],
                z_send.at[step],
                z_recv.at[step],
                (owner * 2 + core, vocab),
            )
        )
        z_copies[-1].start()
        return total

    for step in range(chips + 2):
        if step < chips:
            make(step)
        if 0 <= step - 1 < chips:
            over_vocab(step - 1)
        if 0 <= step - 2 < chips:
            total = over_chips(step - 2)
    for step in range(chips - 1):
        z_copies[step].wait_recv()
        total = total + z_dst[step].astype(jnp.float32)
    out_ref[...] = total
    for copy in pair_copies + list(v_copies.values()) + z_copies:
        copy.wait_send()


def on_device(
    hidden_in,
    attn_gain,
    w_query,
    w_key,
    w_value,
    w_out,
    final_gain,
    teacher_head,
    draft_rows,
    draft_head,
    target_ids,
    rollout_lengths,
    stretch_order,
):
    row_count = hidden_in.shape[0]
    head_dim = HEAD_DIM
    local_heads = w_query.shape[1] // head_dim
    local_groups = w_key.shape[1] // head_dim
    group_size = local_heads // local_groups
    ctx_count = lax.axis_size("ctx")
    chips = ctx_count // 2
    peers = lax.axis_size("vocab")
    bf16, f32, dma = jnp.bfloat16, jnp.float32, pltpu.SemaphoreType.DMA
    half_rows = row_count // 2
    stretch_ids = jnp.arange(stretch_order.shape[0], dtype=jnp.int32)
    rollout_ends = jnp.cumsum(rollout_lengths)

    def locate(begin_row, span_rows):
        row_ids = begin_row + jnp.arange(span_rows, dtype=jnp.int32)
        stretch_hit = (row_ids // half_rows)[:, None] == stretch_ids[None, :]
        stretch_start = jnp.sum(jnp.where(stretch_hit, stretch_order[None, :], 0), axis=1)
        positions = stretch_start * half_rows + row_ids % half_rows
        rollouts = jnp.sum((positions[:, None] >= rollout_ends[None, :]).astype(jnp.int32), axis=1)
        return (positions, rollouts)

    query_pos, query_roll = locate(lax.axis_index("ctx") * row_count, row_count)
    normed = rms_scale(hidden_in.astype(jnp.float32), attn_gain).astype(jnp.bfloat16)
    queries = jnp.dot(normed, w_query, preferred_element_type=jnp.float32).reshape(
        row_count, local_heads, head_dim
    )
    queries = (
        rotate(queries, query_pos)
        .astype(jnp.bfloat16)
        .reshape(row_count, local_groups, group_size, head_dim)
    )
    keys = jnp.dot(normed, w_key, preferred_element_type=jnp.float32).reshape(
        row_count, local_groups, head_dim
    )
    keys = rotate(keys, query_pos).astype(jnp.bfloat16).reshape(row_count, local_groups * head_dim)
    values = jnp.dot(normed, w_value, preferred_element_type=jnp.float32).astype(jnp.bfloat16)
    own = jnp.concatenate([keys, values], axis=1)
    features = draft_rows.shape[1]
    share = row_count // peers
    tokens = row_count * ctx_count
    key_pos, key_roll = locate(jnp.int32(0), tokens)
    attended, draft_all = communicate(
        functools.partial(context_body, chips, peers),
        [
            jax.ShapeDtypeStruct((row_count, local_heads * head_dim), bf16),
            jax.ShapeDtypeStruct((ctx_count, peers, share, features), bf16),
        ],
        (
            own,
            queries.reshape(row_count, local_heads * head_dim),
            query_pos[:, None],
            query_roll[:, None],
            key_pos[None, :],
            key_roll[None, :],
            draft_rows.reshape(peers, share, features),
        ),
        [
            pltpu.VMEM((ctx_count,) + own.shape, bf16),
            pltpu.VMEM((row_count, tokens), f32),
        ]
        + spread_sems(chips, 1)
        + spread_sems(chips, peers),
        0,
    )
    partial_value = jnp.dot(attended, w_out, preferred_element_type=jnp.float32)
    width = hidden_in.shape[1]
    word_count = draft_head.shape[0]
    unit = 2 * row_count
    hops = 1 + (peers - 1) + (chips - 1)
    logits = jax.ShapeDtypeStruct((tokens, word_count), f32)
    teacher_part, draft_part, totals = communicate(
        functools.partial(logits_body, chips, peers),
        [logits, logits, jax.ShapeDtypeStruct((8, tokens), f32)],
        (
            partial_value.reshape(peers, share, width),
            hidden_in.reshape(peers, share, width),
            final_gain.reshape(1, width),
            draft_all,
            teacher_head,
            draft_head,
        ),
        [
            pltpu.VMEM((ctx_count, peers, share, width), bf16),
            pltpu.VMEM((ctx_count, peers, share, features), bf16),
            pltpu.VMEM(teacher_head.shape, bf16),
            pltpu.VMEM(draft_head.shape, bf16),
            pltpu.VMEM((2, unit, word_count), f32),
            pltpu.VMEM((2, unit, 128), f32),
            pltpu.VMEM((3, 8, tokens), f32),
            pltpu.VMEM((hops, 8, tokens), f32),
            pltpu.VMEM((peers - 1, share, width), bf16),
            pltpu.VMEM((peers - 1, share, width), bf16),
            dma((3,)),
            dma((2 * chips,)),
            dma((peers - 1,)),
            dma((peers - 1,)),
            dma((hops,)),
            dma((hops,)),
        ]
        + spread_sems(chips, peers),
        1,
        [pltpu.VMEM] * 3 + [pl.ANY] * 3,
        [pl.ANY, pl.ANY, pltpu.VMEM],
    )
    slice_width = features // peers
    return communicate(
        functools.partial(gradient_body, chips, peers),
        [jax.ShapeDtypeStruct((row_count, slice_width), f32)],
        (
            totals,
            target_ids.astype(f32).reshape(1, tokens),
            teacher_part,
            draft_part,
            draft_head,
        ),
        [
            pltpu.VMEM(draft_head.shape, bf16),
            pltpu.VMEM((2, unit, word_count), f32),
            pltpu.VMEM((2, unit, word_count), f32),
            pltpu.VMEM((unit, word_count), bf16),
            pltpu.VMEM((chips, 2, row_count, features), f32),
            pltpu.VMEM((chips, row_count, features), f32),
            pltpu.VMEM((chips, peers - 1, row_count, slice_width), bf16),
            pltpu.VMEM((chips, peers - 1, row_count, slice_width), bf16),
            pltpu.VMEM((chips - 1, row_count, slice_width), bf16),
            pltpu.VMEM((chips - 1, row_count, slice_width), bf16),
            dma((1,)),
            dma((chips,)),
            dma((chips,)),
            dma((chips,)),
            dma((chips,)),
            dma((chips, peers - 1)),
            dma((chips, peers - 1)),
            dma((chips - 1,)),
            dma((chips - 1,)),
        ],
        2,
        [pltpu.VMEM] * 2 + [pl.ANY] * 3,
    )[0]


def solution(mesh):
    placed = (
        P("ctx", None),
        P(),
        P(None, "vocab"),
        P(None, "vocab"),
        P(None, "vocab"),
        P("vocab", None),
        P(),
        P(("vocab", "ctx"), None),
        P("ctx", None),
        P(("vocab", "ctx"), None),
        P(),
        P(),
        P(),
    )
    return jax.shard_map(
        on_device, mesh=mesh, in_specs=placed, out_specs=P("ctx", "vocab"), check_vma=False
    )
```

```python
import functools

import jax
import jax.numpy as jnp
from jax import lax
from jax.experimental import pallas as pl
from jax.experimental.pallas import tpu as pltpu
from jax.sharding import PartitionSpec as P

HEAD_DIM = 128


EPSILON = 1e-05
ROPE_BASE = 500000.0
MIXING = 0.5
NEGATIVE = -1e30


def rms_scale(values, gain):
    mean_square = jnp.mean(values * values, axis=-1, keepdims=True)
    return values * lax.rsqrt(mean_square + EPSILON) * gain


def rotate(vectors, positions):
    half_dim = vectors.shape[-1] // 2
    exponents = jnp.arange(half_dim, dtype=jnp.float32) * (2.0 / vectors.shape[-1])
    frequencies = jnp.power(ROPE_BASE, -exponents)
    angles = positions.astype(jnp.float32)[:, None] * frequencies[None, :]
    cosine_values = jnp.cos(angles)[:, None, :]
    sine_values = jnp.sin(angles)[:, None, :]
    leading = vectors[..., :half_dim]
    trailing = vectors[..., half_dim:]
    return jnp.concatenate(
        [
            leading * cosine_values - trailing * sine_values,
            trailing * cosine_values + leading * sine_values,
        ],
        axis=-1,
    )


MESH = pl.DeviceIdType.MESH
VMEM_LIMIT = 56 * 1024 * 1024


def place():
    ctx = lax.axis_index("ctx")
    core = ctx % 2
    return ctx, lax.axis_index("vocab"), core, ctx // 2, ctx + 1 - 2 * core


def flip(index, mask):
    bit = 1
    while bit <= mask:
        if mask & bit:
            index = index + bit * (1 - 2 * ((index // bit) % 2))
        bit *= 2
    return index


def greet(devices):
    barrier = pltpu.get_barrier_semaphore()
    for device in devices:
        pl.semaphore_signal(barrier, inc=1, device_id=device, device_id_type=MESH)
    pl.semaphore_wait(barrier, len(devices))


def push(source, target, send, recv, device):
    return pltpu.make_async_remote_copy(
        src_ref=source,
        dst_ref=target,
        send_sem=send,
        recv_sem=recv,
        device_id=device,
        device_id_type=MESH,
    )


class Spread:
    def __init__(self, chips, peers, block, sems):
        self.chips, self.peers, self.block, self.sems = chips, peers, block, sems
        self.bits = [1 << i for i in range(peers.bit_length() - 1)]
        self.orders = (self.bits, self.bits[::-1])
        self.sent = []

    def piece(self, far, mask, half, other=False):
        ctx, vocab, core, chip, sibling = place()
        source = ((chip - far + self.chips) % self.chips) * 2 + (1 - core if other else core)
        return self.block(source, flip(vocab, mask), half)

    def send(self, piece, send, recv, device):
        self.sent.append(push(piece, piece, send, recv, device))
        self.sent[-1].start()

    def arrive(self, piece, sem):
        ctx, vocab, core, chip, sibling = place()
        push(piece, piece, sem, sem, (sibling, vocab)).wait_recv()

    def hand_on(self, far, mask, half):
        ctx, vocab, core, chip, sibling = place()
        z_send, z_recv, v_send, v_recv, s_send, s_recv = self.sems
        piece = self.piece(far, mask, half)
        order = self.orders[half]
        reached = [i for i, bit in enumerate(order) if mask & bit]
        for i in range(reached[-1] + 1 if reached else 0, len(order)):
            self.send(
                piece,
                v_send.at[far, half, mask, i],
                v_recv.at[far, half, mask | order[i]],
                (ctx, flip(vocab, order[i])),
            )
        self.send(
            piece, s_send.at[far, half, mask], s_recv.at[far, half, mask], (sibling, vocab)
        )

    def start(self):
        ctx, vocab, core, chip, sibling = place()
        z_send, z_recv = self.sems[:2]
        for half in (0, 1):
            for far in range(1, self.chips):
                self.send(
                    self.piece(0, 0, half),
                    z_send.at[far, half],
                    z_recv.at[far, half],
                    (((chip + far) % self.chips) * 2 + core, vocab),
                )
            self.hand_on(0, 0, half)

    def steps(self):
        return range(1, self.chips + len(self.bits))

    def step(self, step):
        z_recv, v_recv = self.sems[1], self.sems[3]
        for level in range(0, len(self.bits) + 1):
            far = step - level
            if not 0 <= far < self.chips or (far == 0 and level == 0):
                continue
            for half in (0, 1):
                for mask in [m for m in range(self.peers) if bin(m).count("1") == level]:
                    sem = v_recv.at[far, half, mask] if mask else z_recv.at[far, half]
                    self.arrive(self.piece(far, mask, half), sem)
                    self.hand_on(far, mask, half)

    def collect(self, far):
        for half in (0, 1):
            for mask in range(self.peers):
                self.arrive(self.piece(far, mask, half, True), self.sems[5].at[far, half, mask])

    def finish(self):
        for copy in self.sent:
            copy.wait_send()


def spread_sems(chips, peers):
    dma = pltpu.SemaphoreType.DMA
    depth = max(1, peers.bit_length() - 1)
    return [
        dma((chips, 2)),
        dma((chips, 2)),
        dma((chips, 2, peers, depth)),
        dma((chips, 2, peers)),
        dma((chips, 2, peers)),
        dma((chips, 2, peers)),
    ]


def communicate(body, out_shape, operands, scratch, collective, in_kinds=None, out_kinds=None):
    in_kinds = in_kinds or [pltpu.VMEM] * len(operands)
    out_kinds = out_kinds or [pltpu.VMEM] * len(out_shape)
    return pl.pallas_call(
        body,
        out_shape=out_shape,
        in_specs=[pl.BlockSpec(memory_space=kind) for kind in in_kinds],
        out_specs=[pl.BlockSpec(memory_space=kind) for kind in out_kinds],
        scratch_shapes=scratch,
        compiler_params=pltpu.CompilerParams(
            collective_id=collective, has_side_effects=True, vmem_limit_bytes=VMEM_LIMIT
        ),
    )(*operands)


def halves(rows):
    width = rows.shape[-1] // 2
    return lambda c, v, half: rows.at[c, v, :, half * width : (half + 1) * width]


def context_body(
    chips, peers, own_ref, query_ref, q_pos, q_roll, k_pos, k_roll, draft_ref, w_out,
    part_ref, draft_all, context, mask, attended, w_held, load_sem, *sems,
):
    ctx, vocab, core, chip, sibling = place()
    half_width = own_ref.shape[1] // 2
    tokens = mask.shape[1]
    heads = query_ref.shape[1] // HEAD_DIM
    group_size = heads // (half_width // HEAD_DIM)
    load = pltpu.make_async_copy(w_out, w_held, load_sem.at[0])
    load.start()
    greet(
        [(sibling, vocab)]
        + [(((chip + far) % chips) * 2 + core, vocab) for far in range(1, chips)]
        + [(ctx, (vocab + far) % peers) for far in range(1, peers)]
    )
    context[ctx] = own_ref[...]
    blocks = Spread(
        chips,
        1,
        lambda c, v, half: context.at[c, :, half * half_width : (half + 1) * half_width],
        sems[:6],
    )
    blocks.start()
    draft_all[ctx, vocab] = draft_ref[vocab]
    draft = Spread(chips, peers, halves(draft_all), sems[6:])
    draft.start()
    allowed = (k_pos[...] <= q_pos[...]) & (k_roll[...] == q_roll[...])
    mask[...] = jnp.where(allowed, 1.0, 0.0)
    for step in blocks.steps():
        blocks.step(step)
    pending = list(draft.steps())
    draft.step(pending.pop(0))
    for far in range(chips):
        blocks.collect(far)
    for head in range(heads):
        at = slice(head * HEAD_DIM, (head + 1) * HEAD_DIM)
        begin = (head // group_size) * HEAD_DIM
        keys = context[:, :, begin : begin + HEAD_DIM].reshape(tokens, HEAD_DIM)
        values = context[:, :, half_width + begin : half_width + begin + HEAD_DIM].reshape(
            tokens, HEAD_DIM
        )
        scores = lax.dot_general(
            query_ref[:, at],
            keys,
            (((1,), (1,)), ((), ())),
            preferred_element_type=jnp.float32,
        ) * (HEAD_DIM ** (-0.5))
        scores = jnp.where(mask[...] > 0.0, scores, NEGATIVE)
        weights = jnp.exp(scores - jnp.max(scores, axis=1, keepdims=True))
        weighted = jnp.dot(
            weights.astype(jnp.bfloat16), values, preferred_element_type=jnp.float32
        )
        attended[:, at] = (weighted / jnp.sum(weights, axis=1, keepdims=True)).astype(
            jnp.bfloat16
        )
        if pending and head % 2 == 1:
            draft.step(pending.pop(0))
    load.wait()
    tile = 512

    def over_features(i, carry):
        at = pl.ds(pl.multiple_of(i * tile, tile), tile)
        part_ref[:, at] = jnp.dot(
            attended[...], w_held[:, at], preferred_element_type=jnp.float32
        )
        return carry

    lax.fori_loop(0, part_ref.shape[1] // tile, over_features, 0)
    for step in pending:
        draft.step(step)
    for far in range(chips):
        draft.collect(far)
    blocks.finish()
    draft.finish()


def combine_pairs(former, latter):
    merged = []
    for member in (0, 2):
        highest = jnp.maximum(former[member], latter[member])
        merged += [
            highest,
            former[member + 1] * jnp.exp(former[member] - highest)
            + latter[member + 1] * jnp.exp(latter[member] - highest),
        ]
    return merged


def logits_body(
    chips, peers, part_ref, hidden_ref, gain_ref, draft_from, t_head, d_head,
    t_out, d_out, totals_ref,
    final_all, draft_all, t_words, d_words, slots, columns, held, landed, send_buf, recv_buf,
    load_sem, store_sem, r_send, r_recv, x_send, x_recv, *sems,
):
    ctx, vocab, core, chip, sibling = place()
    stages = [
        [(sibling, vocab)],
        [(ctx, (vocab + far) % peers) for far in range(1, peers)],
        [(((chip + far) % chips) * 2 + core, vocab) for far in range(1, chips)],
    ]
    loads = [
        pltpu.make_async_copy(d_head, d_words, load_sem.at[0]),
        pltpu.make_async_copy(draft_from, draft_all, load_sem.at[1]),
        pltpu.make_async_copy(t_head, t_words, load_sem.at[2]),
    ]
    for load in loads:
        load.start()
    greet(stages[0] + stages[1] + stages[2])
    copies = []
    for far in range(1, peers):
        owner = (vocab + far) % peers
        send_buf[far - 1] = part_ref[owner].astype(jnp.bfloat16)
        copies.append(
            push(
                send_buf.at[far - 1],
                recv_buf.at[far - 1],
                r_send.at[far - 1],
                r_recv.at[far - 1],
                (ctx, owner),
            )
        )
        copies[-1].start()
    teacher = Spread(chips, peers, halves(final_all), sems)

    rows, words = slots.shape[1], slots.shape[2]
    tile = min(words, 512)
    group = 32
    held[...] = jnp.zeros_like(held)
    stores = []

    def multiply(blocks, source_ref, head_ref, out_ref, member, far):
        count = len(stores)
        slot = count % 2
        if blocks is not None:
            blocks.collect(far)
        owner = (chip - far + chips) % chips
        if count >= 2:
            stores[count - 2].wait()

        def over_words(i, carry):
            at = pl.ds(pl.multiple_of(i * tile, tile), tile)
            left = source_ref[pl.ds(owner * 2, 2)].reshape(rows, source_ref.shape[3])
            slots[slot, :, at] = lax.dot_general(
                left,
                head_ref[at, :],
                (((1,), (1,)), ((), ())),
                preferred_element_type=jnp.float32,
            )
            return carry

        lax.fori_loop(0, words // tile, over_words, 0)
        store = pltpu.make_async_copy(
            slots.at[slot],
            out_ref.at[pl.ds(pl.multiple_of(owner * rows, rows), rows)],
            store_sem.at[count],
        )
        store.start()
        stores.append(store)

        def over_rows(i, carry):
            at = pl.ds(pl.multiple_of(i * group, group), group)
            values = slots[slot, at, :]
            highest = jnp.max(values, axis=1, keepdims=True)
            summed = jnp.sum(jnp.exp(values - highest), axis=1, keepdims=True)
            columns[0, at, :] = jnp.broadcast_to(highest, (group, 128))
            columns[1, at, :] = jnp.broadcast_to(summed, (group, 128))
            return carry

        lax.fori_loop(0, rows // group, over_rows, 0)
        lanes = pl.ds(pl.multiple_of(owner * rows, rows), rows)
        for which in (0, 1):
            held[0, member + which : member + which + 1, lanes] = jnp.transpose(columns[which])[:1]

    def draft_unit(far):
        multiply(None, draft_all, d_words, d_out, 2, far)

    def teacher_unit(far):
        multiply(teacher, final_all, t_words, t_out, 0, far)

    loads[0].wait()
    loads[1].wait()
    early = (chips + 1) // 2
    for far in range(early):
        draft_unit(far)
    for copy in copies:
        copy.wait_recv()
    mixed = hidden_ref[vocab].astype(jnp.float32) + part_ref[vocab]
    for far in range(1, peers):
        mixed = mixed + recv_buf[far - 1].astype(jnp.float32)
    final_all[ctx, vocab] = rms_scale(mixed, gain_ref[...]).astype(jnp.bfloat16)
    teacher.start()
    loads[2].wait()
    waiting = list(range(early, chips))
    done = 0
    for step in teacher.steps():
        teacher.step(step)
        if waiting:
            draft_unit(waiting.pop(0))
        if step > len(teacher.bits):
            teacher_unit(done)
            done += 1
    for far in waiting:
        draft_unit(far)
    for far in range(done, chips):
        teacher_unit(far)

    state = [held[0, member : member + 1] for member in range(4)]
    slot, x_copies = 0, []
    for stage, devices in enumerate(stages):
        if stage:
            for member in range(4):
                held[stage, member : member + 1] = state[member]
        begin = slot
        for device in devices:
            x_copies.append(
                push(held.at[stage], landed.at[slot], x_send.at[slot], x_recv.at[slot], device)
            )
            x_copies[-1].start()
            slot += 1
        for at in range(begin, slot):
            x_copies[at].wait_recv()
            state = combine_pairs(
                state, [landed[at, member : member + 1] for member in range(4)]
            )
    totals_ref[...] = jnp.zeros_like(totals_ref)
    for member in range(4):
        totals_ref[member : member + 1] = state[member]
    for copy in copies + x_copies:
        copy.wait_send()
    teacher.finish()
    for store in stores[-2:]:
        store.wait()


def gradient_body(
    chips, peers, totals_ref, target_ref, t_logits, d_logits, d_head, out_ref,
    d_words, t_rows, d_rows, delta, grads, pair, v_src, v_dst, z_src, z_dst,
    load_sem, t_sem, d_sem, p_send, p_recv, v_send, v_recv, z_send, z_recv,
):
    ctx, vocab, core, chip, sibling = place()
    rows, words = t_rows.shape[1], t_rows.shape[2]
    half_rows = rows // 2
    width = out_ref.shape[1]
    features = d_words.shape[1]
    tile = min(features, 512)
    group = 32
    word_start = (vocab * chips * 2 + ctx) * words

    def block_rows(step):
        owner = (chip + step + 1) % chips
        return pl.ds(pl.multiple_of(owner * rows, rows), rows)

    def fetch(step):
        slot = step % 2
        pairs = [
            pltpu.make_async_copy(
                t_logits.at[block_rows(step)], t_rows.at[slot], t_sem.at[step]
            ),
            pltpu.make_async_copy(
                d_logits.at[block_rows(step)], d_rows.at[slot], d_sem.at[step]
            ),
        ]
        for item in pairs:
            item.start()
        return pairs

    fetched = [fetch(0)]
    load = pltpu.make_async_copy(d_head, d_words, load_sem.at[0])
    load.start()
    greet(
        [(sibling, vocab)]
        + [(((chip + far) % chips) * 2 + core, vocab) for far in range(1, chips)]
        + [(ctx, (vocab + far) % peers) for far in range(1, peers)]
    )
    pair_copies, v_copies, z_copies = [], {}, []

    def column(values):
        return jnp.transpose(jnp.broadcast_to(values, (128, rows)))[:, :1]

    def features_of(index):
        return pl.ds(pl.multiple_of(index * width, 128), width)

    def make(step):
        slot = step % 2
        for item in fetched[step]:
            item.wait()
        if step + 1 < chips:
            fetched.append(fetch(step + 1))
        lanes = block_rows(step)
        t_high = column(totals_ref[0:1, lanes])
        t_scale = column((1.0 - MIXING) / totals_ref[1:2, lanes])
        d_high = column(totals_ref[2:3, lanes])
        d_scale = column(1.0 / totals_ref[3:4, lanes])
        target = column(target_ref[0:1, lanes]).astype(jnp.int32)
        ids = word_start + lax.broadcasted_iota(jnp.int32, (group, words), 1)
        for begin in range(0, rows, group):
            at = slice(begin, begin + group)
            soft = jnp.exp(t_rows[slot, at, :] - t_high[at]) * t_scale[at] + jnp.where(
                target[at] == ids, MIXING, 0.0
            )
            drafted = jnp.exp(d_rows[slot, at, :] - d_high[at]) * d_scale[at]
            delta[at, :] = (drafted - soft).astype(jnp.bfloat16)
        if step == 0:
            load.wait()

        def over_features(i, carry):
            at = pl.ds(pl.multiple_of(i * tile, tile), tile)
            product = jnp.dot(delta[...], d_words[:, at], preferred_element_type=jnp.float32)
            grads[step, 0, :, at] = product[:half_rows]
            grads[step, 1, :, at] = product[half_rows:]
            return carry

        lax.fori_loop(0, features // tile, over_features, 0)
        pair_copies.append(
            push(
                grads.at[step, 1 - core],
                pair.at[step],
                p_send.at[step],
                p_recv.at[step],
                (sibling, vocab),
            )
        )
        pair_copies[-1].start()

    def over_vocab(step):
        pair_copies[step].wait_recv()
        for far in range(1, peers):
            at = features_of((vocab + far) % peers)
            v_src[step, far - 1] = (grads[step, core, :, at] + pair[step, :, at]).astype(
                jnp.bfloat16
            )
            v_copies[step, far] = push(
                v_src.at[step, far - 1],
                v_dst.at[step, far - 1],
                v_send.at[step, far - 1],
                v_recv.at[step, far - 1],
                (ctx, (vocab + far) % peers),
            )
            v_copies[step, far].start()

    def over_chips(step):
        at = features_of(vocab)
        total = grads[step, core, :, at] + pair[step, :, at]
        for far in range(1, peers):
            v_copies[step, far].wait_recv()
            total = total + v_dst[step, far - 1].astype(jnp.float32)
        if step == chips - 1:
            return total
        z_src[step] = total.astype(jnp.bfloat16)
        owner = (chip + step + 1) % chips
        z_copies.append(
            push(
                z_src.at[step],
                z_dst.at[step],
                z_send.at[step],
                z_recv.at[step],
                (owner * 2 + core, vocab),
            )
        )
        z_copies[-1].start()
        return total

    for step in range(chips + 2):
        if step < chips:
            make(step)
        if 0 <= step - 1 < chips:
            over_vocab(step - 1)
        if 0 <= step - 2 < chips:
            total = over_chips(step - 2)
    for step in range(chips - 1):
        z_copies[step].wait_recv()
        total = total + z_dst[step].astype(jnp.float32)
    out_ref[...] = total
    for copy in pair_copies + list(v_copies.values()) + z_copies:
        copy.wait_send()


def on_device(
    hidden_in,
    attn_gain,
    w_query,
    w_key,
    w_value,
    w_out,
    final_gain,
    teacher_head,
    draft_rows,
    draft_head,
    target_ids,
    rollout_lengths,
    stretch_order,
):
    row_count = hidden_in.shape[0]
    head_dim = HEAD_DIM
    local_heads = w_query.shape[1] // head_dim
    local_groups = w_key.shape[1] // head_dim
    group_size = local_heads // local_groups
    ctx_count = lax.axis_size("ctx")
    chips = ctx_count // 2
    peers = lax.axis_size("vocab")
    bf16, f32, dma = jnp.bfloat16, jnp.float32, pltpu.SemaphoreType.DMA
    half_rows = row_count // 2
    stretch_ids = jnp.arange(stretch_order.shape[0], dtype=jnp.int32)
    rollout_ends = jnp.cumsum(rollout_lengths)

    def locate(begin_row, span_rows):
        row_ids = begin_row + jnp.arange(span_rows, dtype=jnp.int32)
        stretch_hit = (row_ids // half_rows)[:, None] == stretch_ids[None, :]
        stretch_start = jnp.sum(jnp.where(stretch_hit, stretch_order[None, :], 0), axis=1)
        positions = stretch_start * half_rows + row_ids % half_rows
        rollouts = jnp.sum((positions[:, None] >= rollout_ends[None, :]).astype(jnp.int32), axis=1)
        return (positions, rollouts)

    query_pos, query_roll = locate(lax.axis_index("ctx") * row_count, row_count)
    normed = rms_scale(hidden_in.astype(jnp.float32), attn_gain).astype(jnp.bfloat16)
    queries = jnp.dot(normed, w_query, preferred_element_type=jnp.float32).reshape(
        row_count, local_heads, head_dim
    )
    queries = (
        rotate(queries, query_pos)
        .astype(jnp.bfloat16)
        .reshape(row_count, local_groups, group_size, head_dim)
    )
    keys = jnp.dot(normed, w_key, preferred_element_type=jnp.float32).reshape(
        row_count, local_groups, head_dim
    )
    keys = rotate(keys, query_pos).astype(jnp.bfloat16).reshape(row_count, local_groups * head_dim)
    values = jnp.dot(normed, w_value, preferred_element_type=jnp.float32).astype(jnp.bfloat16)
    own = jnp.concatenate([keys, values], axis=1)
    features = draft_rows.shape[1]
    share = row_count // peers
    tokens = row_count * ctx_count
    key_pos, key_roll = locate(jnp.int32(0), tokens)
    partial_value, draft_all = communicate(
        functools.partial(context_body, chips, peers),
        [
            jax.ShapeDtypeStruct((row_count, w_out.shape[1]), f32),
            jax.ShapeDtypeStruct((ctx_count, peers, share, features), bf16),
        ],
        (
            own,
            queries.reshape(row_count, local_heads * head_dim),
            query_pos[:, None],
            query_roll[:, None],
            key_pos[None, :],
            key_roll[None, :],
            draft_rows.reshape(peers, share, features),
            w_out,
        ),
        [
            pltpu.VMEM((ctx_count,) + own.shape, bf16),
            pltpu.VMEM((row_count, tokens), f32),
            pltpu.VMEM((row_count, local_heads * head_dim), bf16),
            pltpu.VMEM(w_out.shape, bf16),
            dma((1,)),
        ]
        + spread_sems(chips, 1)
        + spread_sems(chips, peers),
        0,
        [pltpu.VMEM] * 7 + [pl.ANY],
    )
    width = hidden_in.shape[1]
    word_count = draft_head.shape[0]
    unit = 2 * row_count
    hops = 1 + (peers - 1) + (chips - 1)
    logits = jax.ShapeDtypeStruct((tokens, word_count), f32)
    teacher_part, draft_part, totals = communicate(
        functools.partial(logits_body, chips, peers),
        [logits, logits, jax.ShapeDtypeStruct((8, tokens), f32)],
        (
            partial_value.reshape(peers, share, width),
            hidden_in.reshape(peers, share, width),
            final_gain.reshape(1, width),
            draft_all,
            teacher_head,
            draft_head,
        ),
        [
            pltpu.VMEM((ctx_count, peers, share, width), bf16),
            pltpu.VMEM((ctx_count, peers, share, features), bf16),
            pltpu.VMEM(teacher_head.shape, bf16),
            pltpu.VMEM(draft_head.shape, bf16),
            pltpu.VMEM((2, unit, word_count), f32),
            pltpu.VMEM((2, unit, 128), f32),
            pltpu.VMEM((3, 8, tokens), f32),
            pltpu.VMEM((hops, 8, tokens), f32),
            pltpu.VMEM((peers - 1, share, width), bf16),
            pltpu.VMEM((peers - 1, share, width), bf16),
            dma((3,)),
            dma((2 * chips,)),
            dma((peers - 1,)),
            dma((peers - 1,)),
            dma((hops,)),
            dma((hops,)),
        ]
        + spread_sems(chips, peers),
        1,
        [pltpu.VMEM] * 3 + [pl.ANY] * 3,
        [pl.ANY, pl.ANY, pltpu.VMEM],
    )
    slice_width = features // peers
    return communicate(
        functools.partial(gradient_body, chips, peers),
        [jax.ShapeDtypeStruct((row_count, slice_width), f32)],
        (
            totals,
            target_ids.astype(f32).reshape(1, tokens),
            teacher_part,
            draft_part,
            draft_head,
        ),
        [
            pltpu.VMEM(draft_head.shape, bf16),
            pltpu.VMEM((2, unit, word_count), f32),
            pltpu.VMEM((2, unit, word_count), f32),
            pltpu.VMEM((unit, word_count), bf16),
            pltpu.VMEM((chips, 2, row_count, features), f32),
            pltpu.VMEM((chips, row_count, features), f32),
            pltpu.VMEM((chips, peers - 1, row_count, slice_width), bf16),
            pltpu.VMEM((chips, peers - 1, row_count, slice_width), bf16),
            pltpu.VMEM((chips - 1, row_count, slice_width), bf16),
            pltpu.VMEM((chips - 1, row_count, slice_width), bf16),
            dma((1,)),
            dma((chips,)),
            dma((chips,)),
            dma((chips,)),
            dma((chips,)),
            dma((chips, peers - 1)),
            dma((chips, peers - 1)),
            dma((chips - 1,)),
            dma((chips - 1,)),
        ],
        2,
        [pltpu.VMEM] * 2 + [pl.ANY] * 3,
    )[0]


def solution(mesh):
    placed = (
        P("ctx", None),
        P(),
        P(None, "vocab"),
        P(None, "vocab"),
        P(None, "vocab"),
        P("vocab", None),
        P(),
        P(("vocab", "ctx"), None),
        P("ctx", None),
        P(("vocab", "ctx"), None),
        P(),
        P(),
        P(),
    )
    return jax.shard_map(
        on_device, mesh=mesh, in_specs=placed, out_specs=P("ctx", "vocab"), check_vma=False
    )
```
